128 devices in a mesh: ctx: 2 (over core), sess: 64 (over z, y, x).
Axes of the slice: x: 4, y: 4, z: 4, core: 2. Of those that a mesh axis runs over, the one named last changes fastest.
Arguments:
- query_rows: bfloat16 [64, 1536, 4096], P('sess', 'ctx'), may hold values from -6 to 6
- key_rows: bfloat16 [64, 1536, 4096], P('sess', 'ctx'), may hold values from -0.59765625 to 0.59765625
- value_rows: bfloat16 [64, 1536, 4096], P('sess', 'ctx'), may hold values from -6 to 6
- decay_rates: float32 [64, 1536, 32], P('sess', 'ctx'), may hold values from 0 to 1, as said below
- valid_blocks: int32 [64], P('sess'), may hold values from 1 to 6, as said below
- step_queries: bfloat16 [2048, 4, 4096], P('sess', None, 'ctx'), may hold values from -6 to 6
- step_keys: bfloat16 [2048, 4, 4096], P('sess', None, 'ctx'), may hold values from -3 to 3
- step_values: bfloat16 [2048, 4, 4096], P('sess', None, 'ctx'), may hold values from -6 to 6
- step_rates: bfloat16 [2048, 4, 32], P('sess', None, 'ctx'), may hold values from 0.019897461 to 0.69921875
- row_session: int32 [2048, 1], P('sess'), may hold values from 0 to 63; in each aligned block of 32 rows (0 to 31, 32 to 63, ...) no two rows name the same one
Outputs:
- prefill_out: bfloat16 [64, 1536, 4096], P('sess', 'ctx')
- decode_out: bfloat16 [2048, 4, 4096], P('sess', None, 'ctx')
The draws below stay inside these ranges and needn't reach their ends.
Inputs may be any that keep to these rules, and one draw needn't show every extreme that they name: The blocks of 256 positions after the first valid_blocks of a session are padding; some session uses all 6. `decay_rates`: decay rates of the heads, positive. `row_session`: among the rows of one index of sess (aligned blocks of 32 rows) no session is named by more than 1 row, a bound that some block reaches; every session is named by some row.
All inputs are finite; a program needn't handle non-finite values.
Results may differ from the reference program's by a relative error of at most 0.0053.
Values may be sent and summed in bfloat16 or wider, within the bound.
A program may use at most 256 MiB of HBM per device.

```python
import math
import jax
import jax.numpy as jnp
import numpy as np
from jax import lax

H = 32
DH = 128
BLK = 256
TOK_DEV = 768
DEC_DEV = 32
STEPS = 4
ROW_MOST = 1
HD = 4096
DIALOG_TOTAL = 64
DIALOG_SPAN = 1536
BLOCKS = 6
ROWS = 2048


def draw_decay_rates(key, part):
    key = jax.random.fold_in(key, 7)
    key_kind, key_fast, key_slow, key_device, key_token, pivotal_token_slot, pivotal_extra_decay = jax.random.split(key, 7)
    fast_share = 0.5
    slow_low = 0.05
    slow_high = 0.5
    fast_heads = jax.random.bernoulli(key_kind, fast_share, (DIALOG_TOTAL, 1, 1, H))
    fast_rate = jnp.exp(jax.random.uniform(key_fast, (DIALOG_TOTAL, 1, 1, H), jnp.float32, math.log(1.0 / 50.0), math.log(1.0 / 30.0)))
    slow_rate = jnp.exp(jax.random.uniform(key_slow, (DIALOG_TOTAL, 1, 1, H), jnp.float32, math.log(slow_low / DIALOG_SPAN), math.log(slow_high / DIALOG_SPAN)))
    head_rate = jnp.where(fast_heads, fast_rate, slow_rate)
    device_factor = jnp.exp(jax.random.uniform(key_device, (DIALOG_TOTAL, DIALOG_SPAN // TOK_DEV, 1, H), jnp.float32, math.log(0.5), math.log(2.0)))
    token_factor = jnp.exp(jax.random.uniform(key_token, (DIALOG_TOTAL, DIALOG_SPAN // TOK_DEV, TOK_DEV, H), jnp.float32, math.log(0.5), math.log(2.0)))
    resting_decays = (head_rate * device_factor * token_factor).reshape(DIALOG_TOTAL, DIALOG_SPAN, H)
    surge_token_slot = jax.random.randint(pivotal_token_slot, (DIALOG_TOTAL, 2, 1), 0, DIALOG_SPAN, dtype=jnp.int32)
    surge_indicator = jnp.any(jnp.arange(DIALOG_SPAN, dtype=jnp.int32)[None, None, :] == surge_token_slot, axis=1)
    surge_extra_decay = -jnp.log(jax.random.uniform(pivotal_extra_decay, (DIALOG_TOTAL, DIALOG_SPAN, 1), jnp.float32, 0.5, 0.8))
    return (resting_decays + jnp.where(surge_indicator[:, :, None], surge_extra_decay, 0.0)).astype(jnp.float32)


def draw_valid_blocks(key, part):
    key = jax.random.fold_in(key, 11)
    key_counts, key_chosen = jax.random.split(key)
    counts = jax.random.randint(key_counts, (DIALOG_TOTAL,), max(1, BLOCKS // 4), BLOCKS + 1, dtype=jnp.int32)
    chosen = jax.random.randint(key_chosen, (), 0, DIALOG_TOTAL, dtype=jnp.int32)
    return jnp.where(jnp.arange(DIALOG_TOTAL, dtype=jnp.int32) == chosen, BLOCKS, counts).astype(jnp.int32)


def block_levels(stream_key, shape, cuts, smallest, largest):
    gain, own = 1.0, jax.random.fold_in(stream_key, 6)
    for position, shards_of in cuts:
        steps = jnp.exp(jax.random.uniform(jax.random.fold_in(own, position), (shards_of,), jnp.float32, smallest / len(cuts), largest / len(cuts)))
        gain = gain * jnp.repeat(steps, shape[position] // shards_of).reshape([-1 if axis == position else 1 for axis in range(len(shape))])
    return gain


def routed_block(key, own, number, rows, amount, top, reach, lean):
    sequence = jax.random.permutation(key, amount)
    crowded, ordinary = load_shares(amount, rows * top, reach, lean, True), load_shares(amount, rows * top, reach, lean, False)
    places = jnp.arange(amount)

    def named(sizes, offset_by):
        used = int((sizes > 0).sum())
        fixed = max(1, used // 4)
        passed = fixed + (places - fixed + offset_by * (used - fixed)) % max(1, amount - fixed)
        return jnp.zeros((amount,), jnp.int32).at[sequence[jnp.where(places < fixed, places, passed)]].set(jnp.asarray(sizes, jnp.int32))

    sizes = jnp.where(number % 4 == 0, named(crowded, number // 4), named(ordinary, number - number // 4 - 1))
    mixed = jax.random.permutation(jax.random.fold_in(own, 3), amount)
    giver, taker = mixed[0:amount // 2 * 2:2], mixed[1:amount // 2 * 2:2]
    slack = jnp.minimum(sizes[giver] - 1, reach - sizes[taker]) // 2
    slack = jnp.where((giver == sequence[0]) | (taker == sequence[0]) | (sizes[taker] == 0), 0, jnp.maximum(slack, 0))
    passed = jax.random.randint(jax.random.fold_in(own, 4), (amount // 2,), 0, 1 << 20) % (slack + 1)
    sizes = sizes.at[giver].add(-passed).at[taker].add(passed)
    members = jnp.searchsorted(jnp.cumsum(sizes), jnp.arange(rows * top), side="right").astype(jnp.int32)
    listing = members.reshape(top, rows).T
    listing = listing[jax.random.permutation(jax.random.fold_in(own, 1), rows)]
    offset_by = jax.random.randint(jax.random.fold_in(own, 2), (rows, 1), 0, top)
    return jnp.take_along_axis(listing, (jnp.arange(top)[None, :] + offset_by) % top, axis=1)


def load_shares(number_of, total, reach, slope, full):
    weights = [(1 << 20) // math.isqrt(standing ** slope) + 1 for standing in range(1, number_of + 1)]
    largest = reach if full else min(reach, max(-(-total // number_of), total * weights[0] // sum(weights)))
    least = 1 if total - largest >= number_of - 1 else 0
    holding, surplus = [largest] + [least] * (number_of - 1), total - largest - least * (number_of - 1)
    while surplus > 0:
        free = [i for i in range(1, number_of) if holding[i] < largest] or [i for i in range(1, number_of) if holding[i] < reach]
        pool, budget = sum([weights[i] for i in free]), surplus
        for i in free:
            more = min(reach - holding[i], max(1, budget * weights[i] // pool), surplus)
            holding[i] = holding[i] + more
            surplus = surplus - more
    return np.array(holding)


def bell_draw(rng, dims, width, limit, cuts=(), kind=jnp.bfloat16):
    values = width * jax.random.normal(rng, dims, jnp.float32)
    if cuts:
        values = values * block_levels(rng, dims, cuts, -0.22, 0.18)
    return jnp.clip(values, -limit, limit).astype(kind)


def setup_inputs(seed: int = 0) -> dict:
    streams_of = jax.random.split(jax.random.key(seed), 11)
    query_rows = bell_draw(streams_of[0], (DIALOG_TOTAL, DIALOG_SPAN, HD), 1.0, 6.0, ((0, 64), (1, 2)))
    key_rows = bell_draw(streams_of[1], (DIALOG_TOTAL, DIALOG_SPAN, HD), 0.09, 0.59765625, ((0, 64), (1, 2)))
    value_rows = bell_draw(streams_of[2], (DIALOG_TOTAL, DIALOG_SPAN, HD), 1.0, 6.0, ((0, 64), (1, 2)))
    decay_rates = draw_decay_rates(jax.random.fold_in(streams_of[10], 71), 0)
    valid_blocks = draw_valid_blocks(jax.random.fold_in(streams_of[10], 71), 0)
    step_queries = bell_draw(streams_of[5], (ROWS, STEPS, HD), 1.0, 6.0, ((0, 64), (2, 2)))
    step_keys = bell_draw(streams_of[6], (ROWS, STEPS, HD), 0.5, 3.0, ((0, 64), (2, 2)))
    step_values = bell_draw(streams_of[7], (ROWS, STEPS, HD), 1.0, 6.0, ((0, 64), (2, 2)))
    step_rates = jnp.clip(jnp.exp(math.log(0.69921875) - 3.5593715 * jax.random.uniform(streams_of[8], (ROWS, STEPS, H), jnp.float32) ** block_levels(streams_of[8], (ROWS, STEPS, H), ((0, 64), (2, 2)), -0.2, 0.2)), 0.019897461, 0.69921875).astype(jnp.bfloat16)
    row_session_keys = jax.random.split(jax.random.fold_in(streams_of[9], 1), ROWS // DEC_DEV)
    row_session_turns = jax.random.permutation(jax.random.fold_in(streams_of[9], 3), ROWS // DEC_DEV)
    row_session = jax.vmap(lambda own, number: routed_block(jax.random.fold_in(streams_of[9], 2), own, number, DEC_DEV, DIALOG_TOTAL, 1, ROW_MOST, 1))(row_session_keys, row_session_turns).reshape((ROWS, 1))
    return dict(query_rows=query_rows, key_rows=key_rows, value_rows=value_rows, decay_rates=decay_rates, valid_blocks=valid_blocks, step_queries=step_queries, step_keys=step_keys, step_values=step_values, step_rates=step_rates, row_session=row_session)


EPSILON = 1e-06

def head_norm(values):
    return values * lax.rsqrt(lax.optimization_barrier(jnp.mean(values * values, axis=-1, keepdims=True)) + EPSILON)

def reference(query_rows, key_rows, value_rows, decay_rates, valid_blocks, step_queries, step_keys, step_values, step_rates, row_session):
    positions = jnp.arange(DIALOG_SPAN, dtype=jnp.int32)
    live_mask = positions[None, :] < (valid_blocks * BLK)[:, None]
    live_rates = jnp.where(live_mask[:, :, None], decay_rates, 0.0)
    masked_keys = jnp.where(live_mask[:, :, None], key_rows, jnp.zeros_like(key_rows))

    def blocked(data):
        return data.reshape(DIALOG_TOTAL, BLOCKS, BLK, H, DH).transpose(1, 0, 3, 2, 4)
    query_blocks = blocked(query_rows)
    key_blocks = blocked(masked_keys)
    value_blocks = blocked(value_rows)
    rate_blocks = live_rates.reshape(DIALOG_TOTAL, BLOCKS, BLK, H).transpose(1, 0, 3, 2)
    causal_mask = jnp.arange(BLK)[:, None] >= jnp.arange(BLK)[None, :]

    def advance(state, inputs):
        queries, keys_part, values_part, rates_part = inputs
        queries_wide = queries.astype(jnp.float32)
        keys_wide = keys_part.astype(jnp.float32)
        values_wide = values_part.astype(jnp.float32)
        running_decay = jnp.cumsum(rates_part, axis=-1)
        block_decay = running_decay[..., -1:]
        scores = jnp.einsum('nhtd,nhsd->nhts', queries_wide, keys_wide)
        decay_gap = running_decay[..., :, None] - running_decay[..., None, :]
        weights = jnp.where(causal_mask, jnp.exp(-jnp.where(causal_mask, decay_gap, 0.0)), 0.0)
        mixed_scores = (scores * weights).astype(jnp.bfloat16)
        within = jnp.einsum('nhts,nhsd->nhtd', mixed_scores.astype(jnp.float32), values_wide)
        entering = lax.optimization_barrier(state.astype(jnp.bfloat16)).astype(jnp.float32)
        across = jnp.exp(-running_decay)[..., None] * jnp.einsum('nhtd,nhde->nhte', queries_wide, entering)
        weighted = (keys_wide * jnp.exp(running_decay - block_decay)[..., None]).astype(jnp.bfloat16)
        increment = jnp.einsum('nhsd,nhse->nhde', weighted.astype(jnp.float32), values_wide)
        new_state = jnp.exp(-block_decay)[..., None] * state + increment
        return (new_state, head_norm(within + across))
    start_state = jnp.zeros((DIALOG_TOTAL, H, DH, DH), jnp.float32)
    final_state, normed = lax.scan(advance, start_state, (query_blocks, key_blocks, value_blocks, rate_blocks))
    normed = normed.transpose(1, 0, 3, 2, 4).reshape(DIALOG_TOTAL, DIALOG_SPAN, H * DH)
    prefill_out = (normed * live_mask[:, :, None]).astype(jnp.bfloat16)

    def decode_one(inputs):
        session_id, queries, keys_part, values_part, rates_part = inputs
        carried = lax.dynamic_index_in_dim(final_state, session_id, 0, keepdims=False)
        readings = []
        for step_index in range(STEPS):
            factor = jnp.exp(-rates_part[step_index].astype(jnp.float32))
            outer_term = keys_part[step_index].astype(jnp.float32)[:, :, None] * values_part[step_index].astype(jnp.float32)[:, None, :]
            carried = factor[:, None, None] * carried + outer_term
            reading = jnp.einsum('hd,hde->he', queries[step_index].astype(jnp.float32), carried, precision=lax.Precision.HIGHEST)
            readings.append(head_norm(reading))
        return jnp.stack(readings).astype(jnp.bfloat16)
    decoded = lax.map(decode_one, (row_session[:, 0].astype(jnp.int32), step_queries.reshape(ROWS, STEPS, H, DH), step_keys.reshape(ROWS, STEPS, H, DH), step_values.reshape(ROWS, STEPS, H, DH), step_rates))
    decode_out = decoded.reshape(ROWS, STEPS, H * DH)
    return (prefill_out, decode_out)
```

```python
import functools

import jax
import jax.numpy as jnp
from jax import lax
from jax.experimental import pallas as pl
from jax.experimental.pallas import tpu as pltpu
from jax.sharding import PartitionSpec as P

BLK = 256
DH = 128
EPSILON = 1e-06
F32 = jnp.float32
BF16 = jnp.bfloat16
HIGH = lax.Precision.HIGHEST


def dot(a, b, dims=((1,), (0,)), precision=None):
    return lax.dot_general(a, b, (dims, ((), ())), precision=precision, preferred_element_type=F32)


def iota(shape, axis):
    return lax.broadcasted_iota(jnp.int32, shape, axis)


def prepare(rates, live, heads):
    lanes = iota((heads, 128), 1)
    copies = (lax.rem(lanes, heads) == iota((heads, 128), 0)).astype(F32)
    lower = (iota((BLK, BLK), 0) >= iota((BLK, BLK), 1)).astype(F32)
    wide = dot(rates * live, copies, precision=HIGH)
    running = dot(lower, wide, precision=HIGH)
    first = running.astype(BF16).astype(F32)
    second = (running - first).astype(BF16).astype(F32)
    third = running - first - second
    group = lax.div(iota((BLK, 128), 1), heads)
    parts = jnp.where(group == 0, first, jnp.where(group == 1, second, jnp.where(group == 2, third, 0.0)))
    return parts.astype(BF16), running.T


def spread_matrix(pair, heads):
    row, lane = iota((128, 2 * DH), 0), iota((128, 2 * DH), 1)
    wanted = pair * 2 + lax.div(lane, DH)
    return ((lax.rem(row, heads) == wanted) & (row < 3 * heads)).astype(F32).astype(BF16)


def live_factor(valid_ref, j, blocks):
    return (lax.axis_index("ctx") * blocks + j < valid_ref[0]).astype(F32)


def states_kernel(heads, blocks, valid_ref, rates_ref, k_ref, v_ref, mid_ref, end_ref, parts_scr):
    pair = pl.program_id(0)

    @pl.when(pair == 0)
    def _():
        for j in range(blocks):
            live = live_factor(valid_ref, j, blocks)
            parts_scr[j], _ = prepare(rates_ref[j * BLK:(j + 1) * BLK, :], live, heads)

    spread = spread_matrix(pair, heads)
    states = [jnp.zeros((DH, DH), F32)] * 2
    total = jnp.zeros((1, 2 * DH), F32)
    for j in range(blocks):
        rows = slice(j * BLK, (j + 1) * BLK)
        live = live_factor(valid_ref, j, blocks)
        running = dot(parts_scr[j], spread)
        last = running[BLK - 1:BLK, :]
        weighted = (k_ref[rows, :].astype(F32) * (jnp.exp(running - last) * live)).astype(BF16)
        decay = jnp.exp(-last)
        total = total + last
        for one in range(2):
            cols = slice(one * DH, (one + 1) * DH)
            if j > 0:
                mid_ref[one, j - 1] = states[one]
            states[one] = decay[:, cols] * states[one] + dot(weighted[:, cols], v_ref[rows, cols], ((0,), (0,)))
    for one in range(2):
        cols = slice(one * DH, (one + 1) * DH)
        end_ref[one, 0:DH, :] = states[one]
        end_ref[one, DH:DH + 8, :] = jnp.broadcast_to(jnp.exp(-total[:, cols]), (8, DH))


def outputs_kernel(heads, blocks, valid_ref, rates_ref, q_ref, k_ref, v_ref, mid_ref, prefix_ref, out_ref, parts_scr, turned_scr):
    pair = pl.program_id(0)

    @pl.when(pair == 0)
    def _():
        for j in range(blocks):
            live = live_factor(valid_ref, j, blocks)
            parts_scr[j], turned = prepare(rates_ref[j * BLK:(j + 1) * BLK, :], live, heads)
            turned_scr[j] = turned[0:heads, :]

    spread = spread_matrix(pair, heads)
    half = BLK // 2
    lower = iota((half, half), 0) >= iota((half, half), 1)
    before = jnp.zeros((1, 2 * DH), F32)
    for j in range(blocks):
        live = live_factor(valid_ref, j, blocks)
        running = dot(parts_scr[j], spread)
        from_start = jnp.exp(-running)
        for one in range(2):
            cols = slice(one * DH, (one + 1) * DH)
            row = turned_scr[j, pl.ds(pair * 2 + one, 1), :]
            run = running[:, cols]
            rows = slice(j * BLK, (j + 1) * BLK)
            q, k, v = q_ref[rows, cols], k_ref[rows, cols], v_ref[rows, cols]
            top, bottom = q[:half], q[half:]
            scores0 = dot(top, k[:half], ((1,), (1,)))
            scores1 = dot(bottom, k, ((1,), (1,)))
            mixed0 = jnp.where(lower, scores0 * jnp.exp(row[:, :half] - run[:half]), 0.0).astype(BF16)
            mixed10 = scores1[:, :half] * jnp.exp(row[:, :half] - run[half:])
            mixed11 = jnp.where(lower, scores1[:, half:] * jnp.exp(row[:, half:] - run[half:]), 0.0)
            mixed1 = jnp.concatenate([mixed10, mixed11], axis=1).astype(BF16)
            within = jnp.concatenate([dot(mixed0, v[:half]), dot(mixed1, v)], axis=0)
            entering = jnp.exp(-before[:, cols]) * prefix_ref[one, 0:DH, :]
            if j > 0:
                entering = entering + mid_ref[one, j - 1]
            mix = within + from_start[:, cols] * dot(q, entering.astype(BF16))
            scale = lax.rsqrt(jnp.mean(mix * mix, axis=1, keepdims=True) + EPSILON) * live
            out_ref[rows, cols] = (mix * scale).astype(BF16)
        before = before + running[BLK - 1:BLK, :]


def project_kernel(x_ref, mine_ref, other_ref, y_ref):
    quad = pl.program_id(0)
    first_core = lax.axis_index("ctx") == 0
    groups = x_ref.shape[0]
    x = x_ref[...].reshape(groups * 16, DH)
    doubled = jnp.concatenate([x, x], axis=1)
    position = lax.div(lax.rem(iota((groups * 16, DH), 0), 16), 4)
    chosen = None
    for two in range(2):
        columns = []
        for one in range(2):
            h = two * 2 + one
            earlier = jnp.where(first_core, mine_ref[h, 0:DH, :], other_ref[h, 0:DH, :])
            latter = jnp.where(first_core, other_ref[h, 0:DH, :], mine_ref[h, 0:DH, :])
            decay = jnp.where(first_core, other_ref[h, DH:DH + 1, :], mine_ref[h, DH:DH + 1, :])
            final = decay * earlier + latter
            upper = final.astype(BF16)
            rest = (final - upper.astype(F32)).astype(BF16)
            columns.append(jnp.concatenate([upper, rest], axis=0))
        product = dot(doubled, jnp.concatenate(columns, axis=1))
        for one in range(2):
            part = product[:, one * DH:(one + 1) * DH]
            chosen = part if chosen is None else jnp.where(position == two * 2 + one, part, chosen)
    y_ref[...] = chosen.astype(BF16).reshape(groups, 16, DH)


def shift_down(value, amount):
    return pltpu.roll(value, amount, 0)


def decode_kernel(q_ref, k_ref, v_ref, p_ref, g_ref, out_ref):
    q, k, v, p = (ref[...].astype(F32) for ref in (q_ref, k_ref, v_ref, p_ref))
    g = g_ref[...]
    reading = g[:, 4:5] * p
    for delta in range(4):
        kd = k if delta == 0 else shift_down(k, delta)
        vd = v if delta == 0 else shift_down(v, delta)
        affinity = jnp.sum(q * kd, axis=1, keepdims=True)
        reading = reading + (affinity * g[:, delta:delta + 1]) * vd
    scale = lax.rsqrt(jnp.mean(reading * reading, axis=1, keepdims=True) + EPSILON)
    out_ref[...] = (reading * scale).astype(BF16)


def local(query_rows, key_rows, value_rows, decay_rates, valid_blocks, step_queries, step_keys, step_values, step_rates, row_session):
    tokens, width = query_rows.shape[1:]
    heads = decay_rates.shape[2]
    blocks = tokens // BLK
    pairs = heads // 2
    queries, keys, values, rates = query_rows[0], key_rows[0], value_rows[0], decay_rates[0]
    smem = pl.BlockSpec(memory_space=pltpu.SMEM)
    pair_block = pl.BlockSpec((tokens, 2 * DH), lambda p: (0, p))
    rate_block = pl.BlockSpec((tokens, heads), lambda p: (0, 0))
    mid_block = pl.BlockSpec((2, blocks - 1, DH, DH), lambda p: (p, 0, 0, 0))
    end_block = pl.BlockSpec((2, DH + 8, DH), lambda p: (p, 0, 0))
    params = pltpu.CompilerParams(vmem_limit_bytes=48 << 20)

    row_count, steps, share = step_queries.shape
    share_heads = share // DH
    sessions = lax.axis_size("sess")

    def by_head(data):
        return data.reshape(row_count, steps, share_heads, DH).transpose(0, 2, 1, 3).reshape(row_count, share_heads * steps, DH)

    named = row_session[:, 0][None, :] == jnp.arange(sessions, dtype=jnp.int32)[:, None]
    place = jnp.sum(jnp.where(named, jnp.arange(row_count, dtype=jnp.int32)[None, :], 0), axis=1)
    q_rows = by_head(step_queries)
    slots = jnp.where(named.any(axis=1)[:, None, None], q_rows[place], 0)
    arrived = lax.all_to_all(slots, "sess", 0, 0, tiled=True)

    mid, end = pl.pallas_call(
        functools.partial(states_kernel, heads, blocks),
        grid=(pairs,),
        out_shape=(jax.ShapeDtypeStruct((heads, blocks - 1, DH, DH), F32), jax.ShapeDtypeStruct((heads, DH + 8, DH), F32)),
        in_specs=[smem, rate_block, pair_block, pair_block],
        out_specs=(mid_block, end_block),
        scratch_shapes=[pltpu.VMEM((blocks, BLK, 128), BF16)],
        compiler_params=params,
    )(valid_blocks, rates, keys, values)
    prefix = lax.ppermute(end, "ctx", [(0, 1)])
    latter = lax.ppermute(end[:share_heads], "ctx", [(1, 0)])
    mine = lax.dynamic_slice_in_dim(end, lax.axis_index("ctx") * share_heads, share_heads, 0)
    other = jnp.where(lax.axis_index("ctx") == 0, latter, prefix[share_heads:])

    state_block = pl.BlockSpec((4, DH + 8, DH), lambda p: (p, 0, 0))
    slot_block = pl.BlockSpec((sessions, 16, DH), lambda p: (0, p, 0))
    projected = pl.pallas_call(
        project_kernel,
        grid=(share_heads // 4,),
        out_shape=jax.ShapeDtypeStruct((sessions, share_heads * steps, DH), BF16),
        in_specs=[slot_block, state_block, state_block],
        out_specs=slot_block,
        compiler_params=params,
    )(arrived, mine, other)
    back = lax.all_to_all(projected, "sess", 0, 0, tiled=True)

    prefill_out = pl.pallas_call(
        functools.partial(outputs_kernel, heads, blocks),
        grid=(pairs,),
        out_shape=jax.ShapeDtypeStruct((tokens, width), BF16),
        in_specs=[smem, rate_block, pair_block, pair_block, pair_block, mid_block, end_block],
        out_specs=pair_block,
        scratch_shapes=[pltpu.VMEM((blocks, BLK, 128), BF16), pltpu.VMEM((blocks, heads, BLK), F32)],
        compiler_params=params,
    )(valid_blocks, rates, queries, keys, values, mid, prefix)

    log_factor = jnp.cumsum(-step_rates.astype(F32), axis=1).transpose(0, 2, 1)
    factors = []
    for delta in range(steps):
        gap = log_factor[:, :, delta:] - log_factor[:, :, :steps - delta]
        factors.append(jnp.pad(jnp.exp(gap), ((0, 0), (0, 0), (delta, 0))))
    factors.append(jnp.exp(log_factor))
    gains = jnp.stack(factors, axis=-1).reshape(row_count * share_heads * steps, steps + 1)

    flat = (row_count * share_heads * steps, DH)
    part = 256
    flat_block = pl.BlockSpec((part, DH), lambda p: (p, 0))
    decoded = pl.pallas_call(
        decode_kernel,
        grid=(flat[0] // part,),
        out_shape=jax.ShapeDtypeStruct(flat, BF16),
        in_specs=[flat_block] * 4 + [pl.BlockSpec((part, steps + 1), lambda p: (p, 0))],
        out_specs=flat_block,
        compiler_params=params,
    )(q_rows.reshape(flat), by_head(step_keys).reshape(flat), by_head(step_values).reshape(flat), back[row_session[:, 0]].reshape(flat), gains)
    decode_out = decoded.reshape(row_count, share_heads, steps, DH).transpose(0, 2, 1, 3).reshape(row_count, steps, share)
    return prefill_out[None], decode_out


def solution(mesh):
    long, step = P("sess", "ctx", None), P("sess", None, "ctx")
    return jax.shard_map(
        local,
        mesh=mesh,
        in_specs=(long, long, long, long, P("sess"), step, step, step, step, P("sess", None)),
        out_specs=(long, step),
        check_vma=False,
    )
```

```python
import functools

import jax
import jax.numpy as jnp
from jax import lax
from jax.experimental import pallas as pl
from jax.experimental.pallas import tpu as pltpu
from jax.sharding import PartitionSpec as P

BLK = 256
DH = 128
EPSILON = 1e-06
F32 = jnp.float32
BF16 = jnp.bfloat16
HIGH = lax.Precision.HIGHEST
MESH = pl.DeviceIdType.MESH


def dot(a, b, dims=((1,), (0,)), precision=None):
    return lax.dot_general(a, b, (dims, ((), ())), precision=precision, preferred_element_type=F32)


def iota(shape, axis):
    return lax.broadcasted_iota(jnp.int32, shape, axis)


def prepare(rates, live, heads):
    lanes = iota((heads, 128), 1)
    copies = (lax.rem(lanes, heads) == iota((heads, 128), 0)).astype(F32)
    lower = (iota((BLK, BLK), 0) >= iota((BLK, BLK), 1)).astype(F32)
    wide = dot(rates * live, copies, precision=HIGH)
    running = dot(lower, wide, precision=HIGH)
    first = running.astype(BF16).astype(F32)
    second = (running - first).astype(BF16).astype(F32)
    third = running - first - second
    group = lax.div(iota((BLK, 128), 1), heads)
    parts = jnp.where(group == 0, first, jnp.where(group == 1, second, jnp.where(group == 2, third, 0.0)))
    return parts.astype(BF16), running.T


def live_factor(valid_ref, j, blocks):
    return (lax.axis_index("ctx") * blocks + j < valid_ref[0]).astype(F32)


def fused_kernel(
    sizes,
    valid_ref, place_ref, session_ref, rates_ref, q_hbm, k_hbm, v_hbm, sq_hbm, sk_hbm, sv_hbm, gains_hbm,
    out_hbm, decoded_ref,
    qb, kb, vb, sq, sk, sv, gains, slots, arrived, projected, back, recent,
    states, other_states, before, decays, other_decays, parts, turned, spread,
    load_sem, store_sem, step_sem, send_sem, recv_sem, back_send_sem, back_recv_sem, pair_send_sem, pair_recv_sem,
):
    heads, blocks, sessions, rows_here, steps, (side_z, side_y, side_x) = sizes
    share = heads // 2
    groups = heads // 4
    core = lax.axis_index("ctx")
    me = lax.axis_index("sess")
    my_x, my_y, my_z = lax.rem(me, side_x), lax.rem(lax.div(me, side_x), side_y), lax.div(me, side_x * side_y)

    def peer(i):
        px = lax.rem(my_x + lax.rem(i, side_x), side_x)
        py = lax.rem(my_y + lax.rem(lax.div(i, side_x), side_y), side_y)
        pz = lax.rem(my_z + lax.div(i, side_x * side_y), side_z)
        return (pz * side_y + py) * side_x + px

    def block_rows(j):
        return pl.ds(pl.multiple_of(j * BLK, BLK), BLK)

    def load(which, hbm, buffer, j):
        return pltpu.make_async_copy(hbm.at[block_rows(j)], buffer.at[block_rows(j)], load_sem.at[which, j])

    def store(j):
        return pltpu.make_async_copy(qb.at[block_rows(j)], out_hbm.at[block_rows(j)], store_sem.at[j])

    small = [
        pltpu.make_async_copy(a, b, step_sem.at[i])
        for i, (a, b) in enumerate(((sq_hbm, sq), (sk_hbm, sk), (sv_hbm, sv), (gains_hbm, gains)))
    ]
    small[0].start()
    for j in range(blocks):
        load(0, k_hbm, kb, j).start()
        load(1, v_hbm, vb, j).start()
    for copy in small[1:]:
        copy.start()
    for j in range(blocks):
        load(2, q_hbm, qb, j).start()

    barrier = pltpu.get_barrier_semaphore()
    pl.semaphore_signal(barrier, inc=1, device_id=(1 - core, me), device_id_type=MESH)

    def greet(i, carry):
        pl.semaphore_signal(barrier, inc=1, device_id=(core, peer(i)), device_id_type=MESH)
        return carry

    lax.fori_loop(1, sessions, greet, 0)

    small[0].wait()

    def fill(s, carry):
        row = place_ref[s]
        slots[s] = jnp.where(row < rows_here, sq[jnp.minimum(row, rows_here - 1)], jnp.zeros(sq.shape[1:], BF16))
        return carry

    lax.fori_loop(0, sessions, fill, 0)
    arrived[me] = slots[me]
    pl.semaphore_wait(barrier, sessions)

    def dispatch(i):
        return pltpu.make_async_remote_copy(
            src_ref=slots.at[peer(i)], dst_ref=arrived.at[me], send_sem=send_sem.at[i], recv_sem=recv_sem.at[i],
            device_id=(core, peer(i)), device_id_type=MESH)

    def give_back(i):
        return pltpu.make_async_remote_copy(
            src_ref=projected.at[peer(i)], dst_ref=back.at[me], send_sem=back_send_sem.at[i], recv_sem=back_recv_sem.at[i],
            device_id=(core, peer(i)), device_id_type=MESH)

    def each_peer(act):
        def lap(i, carry):
            act(i)
            return carry
        lax.fori_loop(1, sessions, lap, 0)

    each_peer(lambda i: dispatch(i).start())

    for j in range(blocks):
        block_parts, block_turned = prepare(rates_ref[j * BLK:(j + 1) * BLK, :], live_factor(valid_ref, j, blocks), heads)
        parts[j] = block_parts
        turned[j] = block_turned[0:heads, :]

    def spread_group(g, carry):
        row, lane = iota((128, 4 * DH), 0), iota((128, 4 * DH), 1)
        wanted = g * 4 + lax.div(lane, DH)
        chosen = (lax.rem(row, heads) == wanted) & (row < 3 * heads)
        spread[:, pl.ds(pl.multiple_of(g * 4 * DH, 4 * DH), 4 * DH)] = chosen.astype(F32).astype(BF16)
        return carry

    lax.fori_loop(0, groups, spread_group, 0)
    states[0] = jnp.zeros(states.shape[1:], F32)
    before[0] = jnp.zeros(before.shape[1:], F32)

    def group_cols(g):
        return pl.ds(pl.multiple_of(g * 4 * DH, 4 * DH), 4 * DH)

    def state_block(j, carry):
        load(0, k_hbm, kb, j).wait()
        load(1, v_hbm, vb, j).wait()
        live = live_factor(valid_ref, j, blocks)

        def state_group(g, carry):
            rows, cols = block_rows(j), group_cols(g)
            running = dot(parts[j], spread[:, cols])
            last = running[BLK - 1:BLK, :]
            weighted = (kb[rows, cols].astype(F32) * (jnp.exp(running - last) * live)).astype(BF16)
            decay = jnp.exp(-last)
            values = vb[rows, cols]
            before[j + 1, :, cols] = before[j, :, cols] + last
            for one in range(4):
                h = g * 4 + one
                lanes = slice(one * DH, (one + 1) * DH)
                grown = dot(weighted[:, lanes], values[:, lanes], ((0,), (0,)))
                states[j + 1, h] = decay[:, lanes] * states[j, h] + grown
            return carry

        return lax.fori_loop(0, groups, state_group, carry)

    lax.fori_loop(0, blocks, state_block, 0)
    for h in range(heads):
        decays[h] = jnp.exp(-before[blocks, :, h * DH:(h + 1) * DH])

    theirs, ours = pl.multiple_of((1 - core) * share, share), pl.multiple_of(core * share, share)
    exchange = [
        pltpu.make_async_remote_copy(
            src_ref=a, dst_ref=b, send_sem=pair_send_sem.at[i], recv_sem=pair_recv_sem.at[i],
            device_id=(1 - core, me), device_id_type=MESH)
        for i, (a, b) in enumerate((
            (decays, other_decays),
            (states.at[blocks, pl.ds(theirs, share)], other_states.at[pl.ds(theirs, share)]),
            (states.at[blocks, pl.ds(ours, share)], other_states.at[pl.ds(ours, share)]),
        ))
    ]
    for copy in exchange:
        copy.start()

    for copy in small[1:]:
        copy.wait()

    def recent_part(p, carry):
        q, k, v = (ref[pl.ds(p * 4, 4)].reshape(4 * share * steps, DH).astype(F32) for ref in (sq, sk, sv))
        rows = pl.ds(pl.multiple_of(p * 4 * share * steps, 4 * share * steps), 4 * share * steps)
        g = gains[rows, :]
        total = None
        for delta in range(steps):
            kd = k if delta == 0 else pltpu.roll(k, delta, 0)
            vd = v if delta == 0 else pltpu.roll(v, delta, 0)
            term = (jnp.sum(q * kd, axis=1, keepdims=True) * g[:, delta:delta + 1]) * vd
            total = term if total is None else total + term
        recent[rows, :] = total
        return carry

    lax.fori_loop(0, rows_here // 4, recent_part, 0)

    for copy in exchange:
        copy.wait()

    half = BLK // 2
    first_core = core == 0

    def output_block(j):
        load(2, q_hbm, qb, j).wait()
        live = live_factor(valid_ref, j, blocks)

        def output_group(g, carry):
            rows, cols = block_rows(j), group_cols(g)
            running = dot(parts[j], spread[:, cols])
            from_start = jnp.exp(-running)
            q4, k4, v4 = qb[rows, cols], kb[rows, cols], vb[rows, cols]
            lower = iota((half, half), 0) >= iota((half, half), 1)
            entry = jnp.exp(-before[j, 0:1, cols])
            for one in range(4):
                h = g * 4 + one
                lanes = slice(one * DH, (one + 1) * DH)
                row = turned[j, pl.ds(h, 1), :]
                run = running[:, lanes]
                q, k, v = q4[:, lanes], k4[:, lanes], v4[:, lanes]
                scores0 = dot(q[:half], k[:half], ((1,), (1,)))
                scores1 = dot(q[half:], k, ((1,), (1,)))
                mixed0 = jnp.where(lower, scores0 * jnp.exp(row[:, :half] - run[:half]), 0.0).astype(BF16)
                mixed10 = scores1[:, :half] * jnp.exp(row[:, :half] - run[half:])
                mixed11 = jnp.where(lower, scores1[:, half:] * jnp.exp(row[:, half:] - run[half:]), 0.0)
                mixed1 = jnp.concatenate([mixed10, mixed11], axis=1).astype(BF16)
                within = jnp.concatenate([dot(mixed0, v[:half]), dot(mixed1, v)], axis=0)
                prefix = jnp.where(first_core, 0.0, entry[:, lanes] * other_states[h])
                entering = (prefix + states[j, h]).astype(BF16)
                mix = within + from_start[:, lanes] * dot(q, entering)
                scale = lax.rsqrt(jnp.mean(mix * mix, axis=1, keepdims=True) + EPSILON) * live
                qb[rows, pl.ds(pl.multiple_of(h * DH, DH), DH)] = (mix * scale).astype(BF16)
            return carry

        lax.fori_loop(0, groups, output_group, 0)
        store(j).start()

    output_block(0)

    each_peer(lambda i: dispatch(i).wait())

    def project(quad, carry):
        part = pl.ds(pl.multiple_of(quad * 16, 16), 16)
        x = arrived[:, part, :].reshape(sessions * 16, DH)
        doubled = jnp.concatenate([x, x], axis=1)
        position = lax.div(lax.rem(iota((sessions * 16, DH), 0), 16), 4)
        chosen = None
        for two in range(2):
            columns = []
            for one in range(2):
                h = core * share + quad * 4 + two * 2 + one
                mine, other = states[blocks, h], other_states[h]
                earlier = jnp.where(first_core, mine, other)
                latter = jnp.where(first_core, other, mine)
                decay = jnp.where(first_core, other_decays[h, 0:1, :], decays[h, 0:1, :])
                final = decay * earlier + latter
                upper = final.astype(BF16)
                rest = (final - upper.astype(F32)).astype(BF16)
                columns.append(jnp.concatenate([upper, rest], axis=0))
            product = dot(doubled, jnp.concatenate(columns, axis=1))
            for one in range(2):
                piece = product[:, one * DH:(one + 1) * DH]
                chosen = piece if chosen is None else jnp.where(position == two * 2 + one, piece, chosen)
        projected[:, part, :] = chosen.astype(BF16).reshape(sessions, 16, DH)
        return carry

    lax.fori_loop(0, share // 4, project, 0)
    back[me] = projected[me]
    each_peer(lambda i: give_back(i).start())

    def other_blocks(j, carry):
        output_block(j)
        return carry

    lax.fori_loop(1, blocks, other_blocks, 0)

    each_peer(lambda i: give_back(i).wait())

    def finish(p, carry):
        rows = pl.ds(pl.multiple_of(p * 4 * share * steps, 4 * share * steps), 4 * share * steps)
        pieces = [back[session_ref[p * 4 + i]].astype(F32) for i in range(4)]
        reading = gains[rows, steps:steps + 1] * jnp.concatenate(pieces, axis=0) + recent[rows, :]
        scale = lax.rsqrt(jnp.mean(reading * reading, axis=1, keepdims=True) + EPSILON)
        decoded_ref[rows, :] = (reading * scale).astype(BF16)
        return carry

    lax.fori_loop(0, rows_here // 4, finish, 0)
    for j in range(blocks):
        store(j).wait()


def local(side, query_rows, key_rows, value_rows, decay_rates, valid_blocks, step_queries, step_keys, step_values, step_rates, row_session):
    tokens, width = query_rows.shape[1:]
    heads = decay_rates.shape[2]
    blocks = tokens // BLK
    row_count, steps, share_width = step_queries.shape
    share = share_width // DH
    sessions = lax.axis_size("sess")

    def by_head(data):
        return data.reshape(row_count, steps, share, DH).transpose(0, 2, 1, 3).reshape(row_count, share * steps, DH)

    named = row_session[:, 0][None, :] == jnp.arange(sessions, dtype=jnp.int32)[:, None]
    place = jnp.min(jnp.where(named, jnp.arange(row_count, dtype=jnp.int32)[None, :], row_count), axis=1)

    log_factor = jnp.cumsum(-step_rates.astype(F32), axis=1).transpose(0, 2, 1)
    factors = []
    for delta in range(steps):
        gap = log_factor[:, :, delta:] - log_factor[:, :, :steps - delta]
        factors.append(jnp.pad(jnp.exp(gap), ((0, 0), (0, 0), (delta, 0))))
    factors.append(jnp.exp(log_factor))
    flat_rows = row_count * share * steps
    gains = jnp.stack(factors, axis=-1).reshape(flat_rows, steps + 1)

    smem = pl.BlockSpec(memory_space=pltpu.SMEM)
    vmem = pl.BlockSpec(memory_space=pltpu.VMEM)
    hbm = pl.BlockSpec(memory_space=pl.ANY)
    slot = (share * steps, DH)
    dma = pltpu.SemaphoreType.DMA
    prefill_out, decoded = pl.pallas_call(
        functools.partial(fused_kernel, (heads, blocks, sessions, row_count, steps, side)),
        out_shape=(jax.ShapeDtypeStruct((tokens, width), BF16), jax.ShapeDtypeStruct((flat_rows, DH), BF16)),
        in_specs=[smem, smem, smem, vmem] + [hbm] * 7,
        out_specs=(hbm, vmem),
        scratch_shapes=[
            pltpu.VMEM((tokens, width), BF16), pltpu.VMEM((tokens, width), BF16), pltpu.VMEM((tokens, width), BF16),
            pltpu.VMEM((row_count,) + slot, BF16), pltpu.VMEM((row_count,) + slot, BF16), pltpu.VMEM((row_count,) + slot, BF16),
            pltpu.VMEM((flat_rows, steps + 1), F32),
            pltpu.VMEM((sessions,) + slot, BF16), pltpu.VMEM((sessions,) + slot, BF16),
            pltpu.VMEM((sessions,) + slot, BF16), pltpu.VMEM((sessions,) + slot, BF16),
            pltpu.VMEM((flat_rows, DH), F32),
            pltpu.VMEM((blocks + 1, heads, DH, DH), F32), pltpu.VMEM((heads, DH, DH), F32),
            pltpu.VMEM((blocks + 1, 8, width), F32), pltpu.VMEM((heads, 8, DH), F32), pltpu.VMEM((heads, 8, DH), F32),
            pltpu.VMEM((blocks, BLK, 128), BF16), pltpu.VMEM((blocks, heads, BLK), F32), pltpu.VMEM((128, width), BF16),
            dma((3, blocks)), dma((blocks,)), dma((4,)), dma((sessions,)), dma((sessions,)), dma((sessions,)), dma((sessions,)),
            dma((3,)), dma((3,)),
        ],
        compiler_params=pltpu.CompilerParams(collective_id=0, has_side_effects=True, vmem_limit_bytes=56 << 20),
    )(valid_blocks, place, row_session[:, 0], decay_rates[0], query_rows[0], key_rows[0], value_rows[0],
      by_head(step_queries), by_head(step_keys), by_head(step_values), gains)
    decode_out = decoded.reshape(row_count, share, steps, DH).transpose(0, 2, 1, 3).reshape(row_count, steps, share_width)
    return prefill_out[None], decode_out


def solution(mesh):
    long, step = P("sess", "ctx", None), P("sess", None, "ctx")
    devices = mesh.shape["sess"]
    side = round(devices ** (1 / 3))
    sides = (side, side, side) if side ** 3 == devices else (1, 1, devices)
    return jax.shard_map(
        functools.partial(local, sides),
        mesh=mesh,
        in_specs=(long, long, long, long, P("sess"), step, step, step, step, P("sess", None)),
        out_specs=(long, step),
        check_vma=False,
    )
```

```python
import functools
import math

import jax
import jax.numpy as jnp
from jax import lax
from jax.experimental import pallas as pl
from jax.experimental.pallas import tpu as pltpu
from jax.sharding import PartitionSpec as P

BLK = 256
DH = 128
SUB = 64
EPSILON = 1e-06
F32 = jnp.float32
BF16 = jnp.bfloat16
MESH = pl.DeviceIdType.MESH
LN2 = math.log(2.0)
EARLY = 8


def dot(a, b, dims=((1,), (0,))):
    return lax.dot_general(a, b, (dims, ((), ())), preferred_element_type=F32)


def iota(shape, axis):
    return lax.broadcasted_iota(jnp.int32, shape, axis)


def split3(value):
    first = value.astype(BF16)
    second = (value - first.astype(F32)).astype(BF16)
    third = (value - first.astype(F32) - second.astype(F32)).astype(BF16)
    return first, second, third


def fused_kernel(
    sizes,
    valid_ref, place_ref, session_ref, rates_ref, step_rates_ref, q_hbm, k_hbm, v_hbm, sq_hbm, sk_hbm, sv_hbm,
    out_ref, decoded_ref,
    qb, kb, vb, sq, sk, sv, slots, arrived, projected, back, recent, carry_gain, gain_table,
    states, other_states, decays, other_decays,
    key_gain, block_gain, entry_gain, row_gain, query_gain, floor, mixed, raw,
    load_sem, step_sem, send_sem, recv_sem, pair_send_sem, pair_recv_sem,
):
    heads, blocks, sessions, rows_here, steps, (side_z, side_y, side_x) = sizes
    share = heads // 2
    groups = heads // 4
    subs = BLK // SUB
    core = lax.axis_index("ctx")
    me = lax.axis_index("sess")
    my_x, my_y, my_z = lax.rem(me, side_x), lax.rem(lax.div(me, side_x), side_y), lax.div(me, side_x * side_y)

    xs = [lax.rem(my_x + d, side_x) for d in range(side_x)]
    ys = [lax.rem(my_y + d, side_y) * side_x for d in range(side_y)]
    zs = [lax.rem(my_z + d, side_z) * (side_x * side_y) for d in range(side_z)]
    peers = [pz + py + px for pz in zs for py in ys for px in xs][1:]

    def block_rows(j):
        return pl.ds(pl.multiple_of(j * BLK, BLK), BLK)

    def load(which, hbm, buffer, j):
        return pltpu.make_async_copy(hbm.at[block_rows(j)], buffer.at[block_rows(j)], load_sem.at[which, j])

    small = [
        pltpu.make_async_copy(a, b, step_sem.at[i])
        for i, (a, b) in enumerate(((sq_hbm, sq), (sk_hbm, sk), (sv_hbm, sv)))
    ]
    small[0].start()
    for j in range(blocks):
        load(0, k_hbm, kb, j).start()
        load(1, v_hbm, vb, j).start()
    for copy in small[1:]:
        copy.start()
    for j in range(blocks):
        load(2, q_hbm, qb, j).start()

    barrier = pltpu.get_barrier_semaphore()
    pl.semaphore_signal(barrier, inc=1, device_id=(1 - core, me), device_id_type=MESH)

    for other in peers:
        pl.semaphore_signal(barrier, inc=1, device_id=(core, other), device_id_type=MESH)

    small[0].wait()

    def fill(s, carry):
        row = place_ref[s]
        slots[s] = jnp.where(row < rows_here, sq[jnp.minimum(row, rows_here - 1)], jnp.zeros(sq.shape[1:], BF16))
        return carry

    lax.fori_loop(0, sessions, fill, 0)
    arrived[me] = slots[me]

    lives = [(core * blocks + j < valid_ref[0]).astype(F32) for j in range(blocks)]
    masked = jnp.concatenate([rates_ref[:, j * BLK:(j + 1) * BLK] * lives[j] for j in range(blocks)], axis=0)
    upper = (iota((BLK, BLK), 0) <= iota((BLK, BLK), 1)).astype(F32).astype(BF16)
    summed = dot(jnp.concatenate(split3(masked), axis=0), upper)
    count = blocks * heads
    running_all = summed[:count] + summed[count:2 * count] + summed[2 * count:]
    lane = iota((heads, BLK), 1)
    passed = jnp.zeros((heads, 1), F32)
    for j in range(blocks):
        running = running_all[j * heads:(j + 1) * heads]
        last = running[:, BLK - 1:BLK]
        key_gain[j] = jnp.exp(running - last) * lives[j]
        block_gain[j] = jnp.broadcast_to(jnp.exp(-last), (heads, DH))
        entry_gain[j] = jnp.broadcast_to(jnp.exp(-passed), (heads, DH))
        passed = passed + last
        centre = None
        for b in range(subs):
            middle = running[:, b * SUB + SUB // 2:b * SUB + SUB // 2 + 1]
            doublings = jnp.round(middle * (1.0 / LN2))
            level = doublings * LN2
            row_gain[j, b] = jnp.exp(running - level)
            query_gain[j, b] = jnp.broadcast_to(jnp.exp2(-doublings), (heads, DH)).astype(BF16).astype(F32)
            centre = level if b == 0 else jnp.where(lane >= b * SUB, level, centre)
        low = (DH * EPSILON) * jnp.exp(2.0 * (running - centre))
        floor[j] = jnp.concatenate([low, jnp.zeros((DH - heads, BLK), F32)], axis=0).T
    for h in range(heads):
        decays[h] = jnp.broadcast_to(entry_gain[blocks - 1, h:h + 1, :] * block_gain[blocks - 1, h:h + 1, :], (8, DH))
    states[0] = jnp.zeros(states.shape[1:], F32)

    per_step = [step_rates_ref[i].astype(F32) for i in range(steps)]
    spans = []
    for delta in range(1, steps + 1):
        spans.append([sum(per_step[max(0, i - delta + 1):i + 1]) for i in range(steps)])
    tables = [
        jnp.concatenate([jnp.exp(-spans[delta - 1][i]) if i >= delta else jnp.zeros_like(per_step[0]) for i in range(steps)], axis=0)
        for delta in range(1, steps)
    ]
    tables.append(jnp.concatenate([jnp.exp(-spans[i][i]) for i in range(steps)], axis=0))
    flat = share * steps
    line = iota((flat, 2 * flat), 0)
    column = lax.rem(iota((flat, 2 * flat), 1), flat)
    pick = (column == lax.rem(line, steps) * share + lax.div(line, steps)).astype(F32).astype(BF16)
    for n, table in enumerate(tables):
        top = table.astype(BF16)
        rest = (table - top.astype(F32)).astype(BF16)
        gain_table[n] = dot(pick, jnp.concatenate([top, rest], axis=0))

    pl.semaphore_wait(barrier, sessions)

    def dispatch(other):
        return pltpu.make_async_remote_copy(
            src_ref=slots.at[other], dst_ref=arrived.at[me], send_sem=send_sem.at[0], recv_sem=recv_sem.at[0],
            device_id=(core, other), device_id_type=MESH)

    def give_back(other):
        return pltpu.make_async_remote_copy(
            src_ref=projected.at[other], dst_ref=back.at[me], send_sem=send_sem.at[1], recv_sem=recv_sem.at[1],
            device_id=(core, other), device_id_type=MESH)

    def wait_all(src, dst, n):
        whole = pltpu.make_async_remote_copy(
            src_ref=src.at[pl.ds(0, sessions - 1)], dst_ref=dst.at[pl.ds(0, sessions - 1)], send_sem=send_sem.at[n],
            recv_sem=recv_sem.at[n], device_id=(core, peers[0]), device_id_type=MESH)
        whole.wait()

    for other in peers:
        dispatch(other).start()

    def group_cols(g):
        return pl.ds(pl.multiple_of(g * 4 * DH, 4 * DH), 4 * DH)

    def state_block(j, carry):
        load(0, k_hbm, kb, j).wait()
        load(1, v_hbm, vb, j).wait()

        def state_group(g, carry):
            rows, cols = block_rows(j), group_cols(g)
            keys, values = kb[rows, cols], vb[rows, cols]
            for one in range(4):
                h = g * 4 + one
                lanes = slice(one * DH, (one + 1) * DH)
                weighted = (keys[:, lanes].T.astype(F32) * key_gain[j, pl.ds(h, 1), :]).astype(BF16)
                states[j + 1, h] = block_gain[j, pl.ds(h, 1), :] * states[j, h] + dot(weighted, values[:, lanes])
            return carry

        return lax.fori_loop(0, groups, state_group, carry)

    lax.fori_loop(0, blocks, state_block, 0)

    theirs, ours = pl.multiple_of((1 - core) * share, share), pl.multiple_of(core * share, share)
    exchange = [
        pltpu.make_async_remote_copy(
            src_ref=a, dst_ref=b, send_sem=pair_send_sem.at[i], recv_sem=pair_recv_sem.at[i],
            device_id=(1 - core, me), device_id_type=MESH)
        for i, (a, b) in enumerate((
            (decays, other_decays),
            (states.at[blocks, pl.ds(theirs, share)], other_states.at[pl.ds(theirs, share)]),
            (states.at[blocks, pl.ds(ours, share)], other_states.at[pl.ds(ours, share)]),
        ))
    ]
    for copy in exchange:
        copy.start()

    for copy in small[1:]:
        copy.wait()
    part = 4 * flat

    def part_rows(p):
        return pl.ds(pl.multiple_of(p * part, part), part)

    def recent_part(p, carry):
        q, k, v = (ref[pl.ds(p * 4, 4)].reshape(part, DH).astype(F32) for ref in (sq, sk, sv))
        own = iota((part, rows_here), 1) == lax.div(iota((part, rows_here), 0), flat) + p * 4

        def gain(n):
            tiled = jnp.concatenate([gain_table[n]] * 4, axis=0)
            return jnp.sum(jnp.where(own, tiled, 0.0), axis=1, keepdims=True)

        total = jnp.sum(q * k, axis=1, keepdims=True) * v
        for delta in range(1, steps):
            affinity = jnp.sum(q * pltpu.roll(k, delta, 0), axis=1, keepdims=True)
            total = total + (affinity * gain(delta - 1)) * pltpu.roll(v, delta, 0)
        recent[part_rows(p), :] = total
        carry_gain[part_rows(p), :] = jnp.broadcast_to(gain(steps - 1), (part, DH))
        return carry

    lax.fori_loop(0, rows_here // 4, recent_part, 0)

    for copy in exchange:
        copy.wait()

    half = BLK // 2
    first_core = core == 0
    per_half = half // SUB

    laps = blocks * groups
    live = [(core * blocks + j < valid_ref[0]).astype(F32) * math.sqrt(DH) for j in range(blocks)]

    def place_of(lap):
        lap = jnp.clip(lap, 0, laps - 1)
        return lax.div(lap, groups), lax.rem(lap, groups)

    def start_scores(lap):
        j, g = place_of(lap)
        rows, cols = block_rows(j), group_cols(g)
        q4, k4 = qb[rows, cols], kb[rows, cols]
        for one in range(4):
            h = g * 4 + one
            lanes = slice(one * DH, (one + 1) * DH)
            q, k = q4[:, lanes], k4[:, lanes]
            for side in range(2):
                here = slice(side * half, (side + 1) * half)
                seen = (side + 1) * half
                scores = dot(q[here], k[:seen], ((1,), (1,)))
                pieces = []
                for b in range(per_half):
                    n = side * per_half + b
                    piece = scores[b * SUB:(b + 1) * SUB] * row_gain[j, n, pl.ds(h, 1), :][:, :seen]
                    causal = iota((SUB, half), 0) + b * SUB >= iota((SUB, half), 1)
                    latest = jnp.where(causal, piece[:, seen - half:], 0.0)
                    scaled = q[here][b * SUB:(b + 1) * SUB].astype(F32) * query_gain[j, n, pl.ds(h, 1), :]
                    pieces.append(jnp.concatenate(([piece[:, :half]] if side else []) + [latest, scaled], axis=1).astype(BF16))
                mixed[one, :, side * 2 * half:side * 2 * half + seen + half] = jnp.concatenate(pieces, axis=0)

    def apply_values(lap):
        j, g = place_of(lap)
        v4 = vb[block_rows(j), group_cols(g)]
        for one in range(4):
            h = g * 4 + one
            v = v4[:, one * DH:(one + 1) * DH]
            prefix = jnp.where(first_core, 0.0, entry_gain[j, pl.ds(h, 1), :] * other_states[h])
            entering = (prefix + states[j, h]).astype(BF16)
            for side in range(2):
                seen = (side + 1) * half
                weights = mixed[one, :, side * 2 * half:side * 2 * half + seen + half]
                raw[one, side * half:(side + 1) * half, :] = dot(weights, jnp.concatenate([v[:seen], entering], axis=0))

    def normalize(lap):
        j, g = place_of(lap)
        alive = jnp.where(j == 0, live[0], live[1])
        for n in range(2, blocks):
            alive = jnp.where(j == n, live[n], alive)
        for one in range(4):
            h = g * 4 + one
            for side in range(2):
                here = slice(side * half, (side + 1) * half)
                mix = raw[one, here, :]
                low = jnp.where(iota((half, DH), 1) == h, floor[j, here, :], 0.0)
                scale = lax.rsqrt(jnp.sum(mix * mix + low, axis=1, keepdims=True)) * alive
                out_ref[pl.ds(pl.multiple_of(j * BLK + side * half, half), half), pl.ds(pl.multiple_of(h * DH, DH), DH)] = (
                    mix * scale).astype(BF16)

    def output_lap(lap, carry):
        normalize(lap - 2)
        apply_values(lap - 1)
        start_scores(lap)
        return carry

    for j in range(blocks):
        load(2, q_hbm, qb, j).wait()
    raw[...] = jnp.zeros(raw.shape, F32)
    mixed[...] = jnp.zeros(mixed.shape, BF16)
    lax.fori_loop(0, EARLY, output_lap, 0)

    wait_all(slots, arrived, 0)

    def project(quad, carry):
        place = pl.ds(pl.multiple_of(quad * 16, 16), 16)
        x = arrived[:, place, :].reshape(sessions * 16, DH)
        doubled = jnp.concatenate([x, x], axis=1)
        position = lax.div(lax.rem(iota((sessions * 16, DH), 0), 16), 4)
        chosen = None
        for two in range(2):
            columns = []
            for one in range(2):
                h = core * share + quad * 4 + two * 2 + one
                mine, other = states[blocks, h], other_states[h]
                earlier = jnp.where(first_core, mine, other)
                latter = jnp.where(first_core, other, mine)
                decay = jnp.where(first_core, other_decays[h, 0:1, :], decays[h, 0:1, :])
                final = decay * earlier + latter
                top = final.astype(BF16)
                rest = (final - top.astype(F32)).astype(BF16)
                columns.append(jnp.concatenate([top, rest], axis=0))
            product = dot(doubled, jnp.concatenate(columns, axis=1))
            for one in range(2):
                piece = product[:, one * DH:(one + 1) * DH]
                chosen = piece if chosen is None else jnp.where(position == two * 2 + one, piece, chosen)
        projected[:, place, :] = chosen.astype(BF16).reshape(sessions, 16, DH)
        return carry

    lax.fori_loop(0, share // 4, project, 0)
    back[me] = projected[me]
    for other in peers:
        give_back(other).start()

    lax.fori_loop(EARLY, laps + 2, output_lap, 0)

    wait_all(projected, back, 1)

    def finish(p, carry):
        rows = part_rows(p)
        pieces = [back[session_ref[p * 4 + i]].astype(F32) for i in range(4)]
        reading = carry_gain[rows, :] * jnp.concatenate(pieces, axis=0) + recent[rows, :]
        scale = lax.rsqrt(jnp.mean(reading * reading, axis=1, keepdims=True) + EPSILON)
        decoded_ref[rows, :] = (reading * scale).astype(BF16)
        return carry

    lax.fori_loop(0, rows_here // 4, finish, 0)


def local(side, query_rows, key_rows, value_rows, decay_rates, valid_blocks, step_queries, step_keys, step_values, step_rates, row_session):
    tokens, width = query_rows.shape[1:]
    heads = decay_rates.shape[2]
    blocks = tokens // BLK
    subs = BLK // SUB
    row_count, steps, share_width = step_queries.shape
    share = share_width // DH
    sessions = lax.axis_size("sess")

    def by_head(data):
        return data.reshape(row_count, steps, share, DH).transpose(0, 2, 1, 3).reshape(row_count, share * steps, DH)

    named = row_session[:, 0][None, :] == jnp.arange(sessions, dtype=jnp.int32)[:, None]
    place = jnp.min(jnp.where(named, jnp.arange(row_count, dtype=jnp.int32)[None, :], row_count), axis=1)
    flat_rows = row_count * share * steps

    smem = pl.BlockSpec(memory_space=pltpu.SMEM)
    vmem = pl.BlockSpec(memory_space=pltpu.VMEM)
    hbm = pl.BlockSpec(memory_space=pl.ANY)
    slot = (share * steps, DH)
    dma = pltpu.SemaphoreType.DMA
    prefill_out, decoded = pl.pallas_call(
        functools.partial(fused_kernel, (heads, blocks, sessions, row_count, steps, side)),
        out_shape=(pltpu.VMEM((tokens, width), BF16), jax.ShapeDtypeStruct((flat_rows, DH), BF16)),
        in_specs=[smem, smem, smem, vmem, vmem] + [hbm] * 6,
        out_specs=(vmem, vmem),
        scratch_shapes=[
            pltpu.VMEM((tokens, width), BF16), pltpu.VMEM((tokens, width), BF16), pltpu.VMEM((tokens, width), BF16),
            pltpu.VMEM((row_count,) + slot, BF16), pltpu.VMEM((row_count,) + slot, BF16), pltpu.VMEM((row_count,) + slot, BF16),
            pltpu.VMEM((sessions,) + slot, BF16), pltpu.VMEM((sessions,) + slot, BF16),
            pltpu.VMEM((sessions,) + slot, BF16), pltpu.VMEM((sessions,) + slot, BF16),
            pltpu.VMEM((flat_rows, DH), F32), pltpu.VMEM((flat_rows, DH), F32), pltpu.VMEM((steps, share * steps, row_count), F32),
            pltpu.VMEM((blocks + 1, heads, DH, DH), F32), pltpu.VMEM((heads, DH, DH), F32),
            pltpu.VMEM((heads, 8, DH), F32), pltpu.VMEM((heads, 8, DH), F32),
            pltpu.VMEM((blocks, heads, BLK), F32), pltpu.VMEM((blocks, heads, DH), F32), pltpu.VMEM((blocks, heads, DH), F32),
            pltpu.VMEM((blocks, subs, heads, BLK), F32), pltpu.VMEM((blocks, subs, heads, DH), F32),
            pltpu.VMEM((blocks, BLK, DH), F32), pltpu.VMEM((4, BLK // 2, 5 * BLK // 2), BF16), pltpu.VMEM((4, BLK, DH), F32),
            dma((3, blocks)), dma((3,)), dma((2,)), dma((2,)), dma((3,)), dma((3,)),
        ],
        compiler_params=pltpu.CompilerParams(collective_id=0, has_side_effects=True, vmem_limit_bytes=48 << 20),
    )(valid_blocks, place, row_session[:, 0], decay_rates[0].T, step_rates.transpose(1, 2, 0), query_rows[0], key_rows[0], value_rows[0],
      by_head(step_queries), by_head(step_keys), by_head(step_values))
    decode_out = decoded.reshape(row_count, share, steps, DH).transpose(0, 2, 1, 3).reshape(row_count, steps, share_width)
    return prefill_out[None], decode_out


def solution(mesh):
    long, step = P("sess", "ctx", None), P("sess", None, "ctx")
    devices = mesh.shape["sess"]
    side = round(devices ** (1 / 3))
    sides = (side, side, side) if side ** 3 == devices else (1, 1, devices)
    return jax.shard_map(
        functools.partial(local, sides),
        mesh=mesh,
        in_specs=(long, long, long, long, P("sess"), step, step, step, step, P("sess", None)),
        out_specs=(long, step),
        check_vma=False,
    )
```

```python
import functools
import math

import jax
import jax.numpy as jnp
from jax import lax
from jax.experimental import pallas as pl
from jax.experimental.pallas import tpu as pltpu
from jax.sharding import PartitionSpec as P

BLK = 256
DH = 128
SUB = 64
EPSILON = 1e-06
F32 = jnp.float32
BF16 = jnp.bfloat16
MESH = pl.DeviceIdType.MESH
LN2 = math.log(2.0)
EARLY = 4


def dot(a, b, dims=((1,), (0,))):
    return lax.dot_general(a, b, (dims, ((), ())), preferred_element_type=F32)


def iota(shape, axis):
    return lax.broadcasted_iota(jnp.int32, shape, axis)


def split3(value):
    first = value.astype(BF16)
    second = (value - first.astype(F32)).astype(BF16)
    third = (value - first.astype(F32) - second.astype(F32)).astype(BF16)
    return first, second, third


def far_first(side_x, side_y, side_z):
    sides = (side_x, side_y, side_z)

    def hops(offset):
        return sum(min(d, n - d) for d, n in zip(offset, sides))

    def orbit(offset):
        turned = [offset]
        if side_x == side_y == side_z:
            turned += [offset[1:] + offset[:1], offset[2:] + offset[:2]]
        for one in turned:
            yield one
            yield tuple((n - d) % n for d, n in zip(one, sides))

    every = [(a, b, c) for a in range(side_x) for b in range(side_y) for c in range(side_z)][1:]
    order = []
    for offset in sorted(every, key=lambda o: (-hops(o), o)):
        for one in orbit(offset):
            if one not in order:
                order.append(one)
    return order


def fused_kernel(
    sizes,
    valid_ref, place_ref, session_ref, rates_hbm, step_rates_hbm, q_hbm, k_hbm, v_hbm, sq_hbm, sk_hbm, sv_hbm,
    out_ref, decoded_ref,
    qb, kb, vb, rates_ref, step_rates_ref, sq, sk, sv, slots, arrived, projected, back, recent, carry_gain, gain_table,
    states, other_states, decays, other_decays,
    key_gain, block_gain, entry_gain, row_gain, query_gain, floor, mixed, raw,
    load_sem, step_sem, send_sem, recv_sem, pair_send_sem, pair_recv_sem,
):
    heads, blocks, sessions, rows_here, steps, (side_z, side_y, side_x) = sizes
    share = heads // 2
    groups = heads // 4
    subs = BLK // SUB
    core = lax.axis_index("ctx")
    me = lax.axis_index("sess")
    my_x, my_y, my_z = lax.rem(me, side_x), lax.rem(lax.div(me, side_x), side_y), lax.div(me, side_x * side_y)

    xs = [lax.rem(my_x + d, side_x) for d in range(side_x)]
    ys = [lax.rem(my_y + d, side_y) * side_x for d in range(side_y)]
    zs = [lax.rem(my_z + d, side_z) * (side_x * side_y) for d in range(side_z)]
    peers = [zs[c] + ys[b] + xs[a] for a, b, c in far_first(side_x, side_y, side_z)]

    def block_rows(j):
        return pl.ds(pl.multiple_of(j * BLK, BLK), BLK)

    def load(which, hbm, buffer, j):
        return pltpu.make_async_copy(hbm.at[block_rows(j)], buffer.at[block_rows(j)], load_sem.at[which, j])

    small = [
        pltpu.make_async_copy(a, b, step_sem.at[i])
        for i, (a, b) in enumerate(((sq_hbm, sq), (rates_hbm, rates_ref), (step_rates_hbm, step_rates_ref), (sk_hbm, sk), (sv_hbm, sv)))
    ]
    for copy in small[:3]:
        copy.start()
    for j in range(blocks):
        load(0, k_hbm, kb, j).start()
        load(1, v_hbm, vb, j).start()
    for copy in small[3:]:
        copy.start()
    for j in range(blocks):
        load(2, q_hbm, qb, j).start()

    barrier = pltpu.get_barrier_semaphore()
    pl.semaphore_signal(barrier, inc=1, device_id=(1 - core, me), device_id_type=MESH)

    for other in peers:
        pl.semaphore_signal(barrier, inc=1, device_id=(core, other), device_id_type=MESH)

    small[0].wait()

    def fill(s, carry):
        row = place_ref[s]
        slots[s] = jnp.where(row < rows_here, sq[jnp.minimum(row, rows_here - 1)], jnp.zeros(sq.shape[1:], BF16))
        return carry

    lax.fori_loop(0, sessions, fill, 0)
    arrived[me] = slots[me]

    for copy in small[1:3]:
        copy.wait()
    lives = [(core * blocks + j < valid_ref[0]).astype(F32) for j in range(blocks)]
    masked = jnp.concatenate([rates_ref[:, j * BLK:(j + 1) * BLK] * lives[j] for j in range(blocks)], axis=0)
    upper = (iota((BLK, BLK), 0) <= iota((BLK, BLK), 1)).astype(F32).astype(BF16)
    summed = dot(jnp.concatenate(split3(masked), axis=0), upper)
    count = blocks * heads
    running_all = summed[:count] + summed[count:2 * count] + summed[2 * count:]
    lane = iota((heads, BLK), 1)
    passed = jnp.zeros((heads, 1), F32)
    for j in range(blocks):
        running = running_all[j * heads:(j + 1) * heads]
        last = running[:, BLK - 1:BLK]
        key_gain[j] = jnp.exp(running - last) * lives[j]
        block_gain[j] = jnp.broadcast_to(jnp.exp(-last), (heads, DH))
        entry_gain[j] = jnp.broadcast_to(jnp.exp(-passed), (heads, DH))
        passed = passed + last
        centre = None
        for b in range(subs):
            middle = running[:, b * SUB + SUB // 2:b * SUB + SUB // 2 + 1]
            doublings = jnp.round(middle * (1.0 / LN2))
            level = doublings * LN2
            row_gain[j, b] = jnp.exp(running - level)
            query_gain[j, b] = jnp.broadcast_to(jnp.exp2(-doublings), (heads, DH)).astype(BF16).astype(F32)
            centre = level if b == 0 else jnp.where(lane >= b * SUB, level, centre)
        low = (DH * EPSILON) * jnp.exp(2.0 * (running - centre))
        floor[j] = jnp.concatenate([low, jnp.zeros((DH - heads, BLK), F32)], axis=0).T
    for h in range(heads):
        decays[h] = jnp.broadcast_to(entry_gain[blocks - 1, h:h + 1, :] * block_gain[blocks - 1, h:h + 1, :], (8, DH))
    states[0] = jnp.zeros(states.shape[1:], F32)

    per_step = [step_rates_ref[i].astype(F32) for i in range(steps)]
    spans = []
    for delta in range(1, steps + 1):
        spans.append([sum(per_step[max(0, i - delta + 1):i + 1]) for i in range(steps)])
    tables = [
        jnp.concatenate([jnp.exp(-spans[delta - 1][i]) if i >= delta else jnp.zeros_like(per_step[0]) for i in range(steps)], axis=0)
        for delta in range(1, steps)
    ]
    tables.append(jnp.concatenate([jnp.exp(-spans[i][i]) for i in range(steps)], axis=0))
    flat = share * steps
    line = iota((flat, 2 * flat), 0)
    column = lax.rem(iota((flat, 2 * flat), 1), flat)
    pick = (column == lax.rem(line, steps) * share + lax.div(line, steps)).astype(F32).astype(BF16)
    for n, table in enumerate(tables):
        top = table.astype(BF16)
        rest = (table - top.astype(F32)).astype(BF16)
        gain_table[n] = dot(pick, jnp.concatenate([top, rest], axis=0))

    pl.semaphore_wait(barrier, sessions)

    def dispatch(other):
        return pltpu.make_async_remote_copy(
            src_ref=slots.at[other], dst_ref=arrived.at[me], send_sem=send_sem.at[0], recv_sem=recv_sem.at[0],
            device_id=(core, other), device_id_type=MESH)

    def give_back(other):
        return pltpu.make_async_remote_copy(
            src_ref=projected.at[other], dst_ref=back.at[me], send_sem=send_sem.at[1], recv_sem=recv_sem.at[1],
            device_id=(core, other), device_id_type=MESH)

    def wait_all(src, dst, n):
        whole = pltpu.make_async_remote_copy(
            src_ref=src.at[pl.ds(0, sessions - 1)], dst_ref=dst.at[pl.ds(0, sessions - 1)], send_sem=send_sem.at[n],
            recv_sem=recv_sem.at[n], device_id=(core, peers[0]), device_id_type=MESH)
        whole.wait()

    for other in peers:
        dispatch(other).start()

    def group_cols(g):
        return pl.ds(pl.multiple_of(g * 4 * DH, 4 * DH), 4 * DH)

    def state_block(j, carry):
        load(0, k_hbm, kb, j).wait()
        load(1, v_hbm, vb, j).wait()

        def state_group(g, carry):
            rows, cols = block_rows(j), group_cols(g)
            keys, values = kb[rows, cols], vb[rows, cols]
            for one in range(4):
                h = g * 4 + one
                lanes = slice(one * DH, (one + 1) * DH)
                weighted = (keys[:, lanes].T.astype(F32) * key_gain[j, pl.ds(h, 1), :]).astype(BF16)
                states[j + 1, h] = block_gain[j, pl.ds(h, 1), :] * states[j, h] + dot(weighted, values[:, lanes])
            return carry

        return lax.fori_loop(0, groups, state_group, carry)

    lax.fori_loop(0, blocks, state_block, 0)

    theirs, ours = pl.multiple_of((1 - core) * share, share), pl.multiple_of(core * share, share)
    exchange = [
        pltpu.make_async_remote_copy(
            src_ref=a, dst_ref=b, send_sem=pair_send_sem.at[i], recv_sem=pair_recv_sem.at[i],
            device_id=(1 - core, me), device_id_type=MESH)
        for i, (a, b) in enumerate((
            (decays, other_decays),
            (states.at[blocks, pl.ds(theirs, share)], other_states.at[pl.ds(theirs, share)]),
            (states.at[blocks, pl.ds(ours, share)], other_states.at[pl.ds(ours, share)]),
        ))
    ]
    for copy in exchange:
        copy.start()

    for copy in small[3:]:
        copy.wait()
    part = 4 * flat

    def part_rows(p):
        return pl.ds(pl.multiple_of(p * part, part), part)

    def recent_part(p, carry):
        q, k, v = (ref[pl.ds(p * 4, 4)].reshape(part, DH).astype(F32) for ref in (sq, sk, sv))
        own = iota((part, rows_here), 1) == lax.div(iota((part, rows_here), 0), flat) + p * 4

        def gain(n):
            tiled = jnp.concatenate([gain_table[n]] * 4, axis=0)
            return jnp.sum(jnp.where(own, tiled, 0.0), axis=1, keepdims=True)

        total = jnp.sum(q * k, axis=1, keepdims=True) * v
        for delta in range(1, steps):
            affinity = jnp.sum(q * pltpu.roll(k, delta, 0), axis=1, keepdims=True)
            total = total + (affinity * gain(delta - 1)) * pltpu.roll(v, delta, 0)
        recent[part_rows(p), :] = total
        carry_gain[part_rows(p), :] = jnp.broadcast_to(gain(steps - 1), (part, DH))
        return carry

    lax.fori_loop(0, rows_here // 4, recent_part, 0)

    for copy in exchange:
        copy.wait()

    half = BLK // 2
    first_core = core == 0
    per_half = half // SUB

    laps = blocks * groups
    live = [(core * blocks + j < valid_ref[0]).astype(F32) * math.sqrt(DH) for j in range(blocks)]

    def place_of(lap):
        lap = jnp.clip(lap, 0, laps - 1)
        return lax.div(lap, groups), lax.rem(lap, groups)

    def start_scores(lap):
        j, g = place_of(lap)
        rows, cols = block_rows(j), group_cols(g)
        q4, k4 = qb[rows, cols], kb[rows, cols]
        for one in range(4):
            h = g * 4 + one
            lanes = slice(one * DH, (one + 1) * DH)
            q, k = q4[:, lanes], k4[:, lanes]
            for side in range(2):
                here = slice(side * half, (side + 1) * half)
                seen = (side + 1) * half
                scores = dot(q[here], k[:seen], ((1,), (1,)))
                pieces = []
                for b in range(per_half):
                    n = side * per_half + b
                    piece = scores[b * SUB:(b + 1) * SUB] * row_gain[j, n, pl.ds(h, 1), :][:, :seen]
                    causal = iota((SUB, half), 0) + b * SUB >= iota((SUB, half), 1)
                    latest = jnp.where(causal, piece[:, seen - half:], 0.0)
                    scaled = q[here][b * SUB:(b + 1) * SUB].astype(F32) * query_gain[j, n, pl.ds(h, 1), :]
                    pieces.append(jnp.concatenate(([piece[:, :half]] if side else []) + [latest, scaled], axis=1).astype(BF16))
                mixed[one, :, side * 2 * half:side * 2 * half + seen + half] = jnp.concatenate(pieces, axis=0)

    def apply_values(lap):
        j, g = place_of(lap)
        v4 = vb[block_rows(j), group_cols(g)]
        for one in range(4):
            h = g * 4 + one
            v = v4[:, one * DH:(one + 1) * DH]
            prefix = jnp.where(first_core, 0.0, entry_gain[j, pl.ds(h, 1), :] * other_states[h])
            entering = (prefix + states[j, h]).astype(BF16)
            for side in range(2):
                seen = (side + 1) * half
                weights = mixed[one, :, side * 2 * half:side * 2 * half + seen + half]
                raw[one, side * half:(side + 1) * half, :] = dot(weights, jnp.concatenate([v[:seen], entering], axis=0))

    def normalize(lap):
        j, g = place_of(lap)
        alive = jnp.where(j == 0, live[0], live[1])
        for n in range(2, blocks):
            alive = jnp.where(j == n, live[n], alive)
        for one in range(4):
            h = g * 4 + one
            for side in range(2):
                here = slice(side * half, (side + 1) * half)
                mix = raw[one, here, :]
                low = jnp.where(iota((half, DH), 1) == h, floor[j, here, :], 0.0)
                scale = lax.rsqrt(jnp.sum(mix * mix + low, axis=1, keepdims=True)) * alive
                out_ref[pl.ds(pl.multiple_of(j * BLK + side * half, half), half), pl.ds(pl.multiple_of(h * DH, DH), DH)] = (
                    mix * scale).astype(BF16)

    def output_lap(lap, carry):
        normalize(lap - 2)
        apply_values(lap - 1)
        start_scores(lap)
        return carry

    for j in range(blocks):
        load(2, q_hbm, qb, j).wait()
    raw[...] = jnp.zeros(raw.shape, F32)
    mixed[...] = jnp.zeros(mixed.shape, BF16)
    lax.fori_loop(0, EARLY, output_lap, 0)

    wait_all(slots, arrived, 0)

    def project(quad, carry):
        place = pl.ds(pl.multiple_of(quad * 16, 16), 16)
        x = arrived[:, place, :].reshape(sessions * 16, DH)
        doubled = jnp.concatenate([x, x], axis=1)
        position = lax.div(iota((1, 16, DH), 1), 4)
        chosen = None
        for two in range(2):
            columns = []
            for one in range(2):
                h = core * share + quad * 4 + two * 2 + one
                mine, other = states[blocks, h], other_states[h]
                earlier = jnp.where(first_core, mine, other)
                latter = jnp.where(first_core, other, mine)
                decay = jnp.where(first_core, other_decays[h, 0:1, :], decays[h, 0:1, :])
                final = decay * earlier + latter
                top = final.astype(BF16)
                rest = (final - top.astype(F32)).astype(BF16)
                columns.append(jnp.concatenate([top, rest], axis=0))
            product = dot(doubled, jnp.concatenate(columns, axis=1))
            for one in range(2):
                piece = product[:, one * DH:(one + 1) * DH].reshape(sessions, 16, DH)
                chosen = piece if chosen is None else jnp.where(position == two * 2 + one, piece, chosen)
        projected[:, place, :] = chosen.astype(BF16)
        return carry

    lax.fori_loop(0, share // 4, project, 0)
    back[me] = projected[me]
    for other in peers:
        give_back(other).start()

    lax.fori_loop(EARLY, laps + 2, output_lap, 0)

    wait_all(projected, back, 1)

    def finish(p, carry):
        rows = part_rows(p)
        pieces = [back[session_ref[p * 4 + i]].astype(F32) for i in range(4)]
        reading = carry_gain[rows, :] * jnp.concatenate(pieces, axis=0) + recent[rows, :]
        scale = lax.rsqrt(jnp.mean(reading * reading, axis=1, keepdims=True) + EPSILON)
        decoded_ref[rows, :] = (reading * scale).astype(BF16)
        return carry

    lax.fori_loop(0, rows_here // 4, finish, 0)


def local(side, query_rows, key_rows, value_rows, decay_rates, valid_blocks, step_queries, step_keys, step_values, step_rates, row_session):
    tokens, width = query_rows.shape[1:]
    heads = decay_rates.shape[2]
    blocks = tokens // BLK
    subs = BLK // SUB
    row_count, steps, share_width = step_queries.shape
    share = share_width // DH
    sessions = lax.axis_size("sess")

    def by_head(data):
        return data.reshape(row_count, steps, share, DH).transpose(0, 2, 1, 3).reshape(row_count, share * steps, DH)

    named = row_session[:, 0][None, :] == jnp.arange(sessions, dtype=jnp.int32)[:, None]
    place = jnp.min(jnp.where(named, jnp.arange(row_count, dtype=jnp.int32)[None, :], row_count), axis=1)
    flat_rows = row_count * share * steps

    smem = pl.BlockSpec(memory_space=pltpu.SMEM)
    vmem = pl.BlockSpec(memory_space=pltpu.VMEM)
    hbm = pl.BlockSpec(memory_space=pl.ANY)
    slot = (share * steps, DH)
    dma = pltpu.SemaphoreType.DMA
    prefill_out, decoded = pl.pallas_call(
        functools.partial(fused_kernel, (heads, blocks, sessions, row_count, steps, side)),
        out_shape=(pltpu.VMEM((tokens, width), BF16), pltpu.VMEM((flat_rows, DH), BF16)),
        in_specs=[smem, smem, smem] + [hbm] * 8,
        out_specs=(vmem, vmem),
        scratch_shapes=[
            pltpu.VMEM((tokens, width), BF16), pltpu.VMEM((tokens, width), BF16), pltpu.VMEM((tokens, width), BF16),
            pltpu.VMEM((heads, tokens), F32), pltpu.VMEM((steps, share, row_count), BF16),
            pltpu.VMEM((row_count,) + slot, BF16), pltpu.VMEM((row_count,) + slot, BF16), pltpu.VMEM((row_count,) + slot, BF16),
            pltpu.VMEM((sessions,) + slot, BF16), pltpu.VMEM((sessions,) + slot, BF16),
            pltpu.VMEM((sessions,) + slot, BF16), pltpu.VMEM((sessions,) + slot, BF16),
            pltpu.VMEM((flat_rows, DH), F32), pltpu.VMEM((flat_rows, DH), F32), pltpu.VMEM((steps, share * steps, row_count), F32),
            pltpu.VMEM((blocks + 1, heads, DH, DH), F32), pltpu.VMEM((heads, DH, DH), F32),
            pltpu.VMEM((heads, 8, DH), F32), pltpu.VMEM((heads, 8, DH), F32),
            pltpu.VMEM((blocks, heads, BLK), F32), pltpu.VMEM((blocks, heads, DH), F32), pltpu.VMEM((blocks, heads, DH), F32),
            pltpu.VMEM((blocks, subs, heads, BLK), F32), pltpu.VMEM((blocks, subs, heads, DH), F32),
            pltpu.VMEM((blocks, BLK, DH), F32), pltpu.VMEM((4, BLK // 2, 5 * BLK // 2), BF16), pltpu.VMEM((4, BLK, DH), F32),
            dma((3, blocks)), dma((5,)), dma((2,)), dma((2,)), dma((3,)), dma((3,)),
        ],
        compiler_params=pltpu.CompilerParams(collective_id=0, has_side_effects=True, vmem_limit_bytes=48 << 20),
    )(valid_blocks, place, row_session[:, 0], decay_rates[0].T, step_rates.transpose(1, 2, 0), query_rows[0], key_rows[0], value_rows[0],
      by_head(step_queries), by_head(step_keys), by_head(step_values))
    decode_out = decoded.reshape(row_count, share, steps, DH).transpose(0, 2, 1, 3).reshape(row_count, steps, share_width)
    return prefill_out[None], decode_out


def solution(mesh):
    long, step = P("sess", "ctx", None), P("sess", None, "ctx")
    devices = mesh.shape["sess"]
    side = round(devices ** (1 / 3))
    sides = (side, side, side) if side ** 3 == devices else (1, 1, devices)
    return jax.shard_map(
        functools.partial(local, sides),
        mesh=mesh,
        in_specs=(long, long, long, long, P("sess"), step, step, step, step, P("sess", None)),
        out_specs=(long, step),
        check_vma=False,
    )
```

```python
import functools
import math

import jax
import jax.numpy as jnp
from jax import lax
from jax.experimental import pallas as pl
from jax.experimental.pallas import tpu as pltpu
from jax.sharding import PartitionSpec as P

BLK = 256
DH = 128
SUB = 64
EPSILON = 1e-06
F32 = jnp.float32
BF16 = jnp.bfloat16
MESH = pl.DeviceIdType.MESH
LN2 = math.log(2.0)
EARLY = 3


def dot(a, b, dims=((1,), (0,))):
    return lax.dot_general(a, b, (dims, ((), ())), preferred_element_type=F32)


def iota(shape, axis):
    return lax.broadcasted_iota(jnp.int32, shape, axis)


def split3(value):
    first = value.astype(BF16)
    second = (value - first.astype(F32)).astype(BF16)
    third = (value - first.astype(F32) - second.astype(F32)).astype(BF16)
    return first, second, third


def far_first(side_x, side_y, side_z):
    sides = (side_x, side_y, side_z)

    def hops(offset):
        return sum(min(d, n - d) for d, n in zip(offset, sides))

    def orbit(offset):
        turned = [offset]
        if side_x == side_y == side_z:
            turned += [offset[1:] + offset[:1], offset[2:] + offset[:2]]
        for one in turned:
            yield one
            yield tuple((n - d) % n for d, n in zip(one, sides))

    every = [(a, b, c) for a in range(side_x) for b in range(side_y) for c in range(side_z)][1:]
    order = []
    for offset in sorted(every, key=lambda o: (-hops(o), o)):
        for one in orbit(offset):
            if one not in order:
                order.append(one)
    return order


def fused_kernel(
    sizes,
    valid_ref, place_ref, session_ref, rates_hbm, step_rates_hbm, q_hbm, k_hbm, v_hbm, sq_hbm, sk_hbm, sv_hbm,
    out_ref, decoded_ref,
    qb, kb, vb, rates_ref, step_rates_ref, sq, sk, sv, slots, arrived, projected, back, recent, carry_gain, gain_table,
    states, other_states, decays, other_decays,
    key_gain, block_gain, entry_gain, row_gain, query_gain, floor, mixed, raw,
    load_sem, step_sem, send_sem, recv_sem, pair_send_sem, pair_recv_sem,
):
    heads, blocks, sessions, rows_here, steps, (side_z, side_y, side_x) = sizes
    share = heads // 2
    groups = heads // 4
    subs = BLK // SUB
    core = lax.axis_index("ctx")
    me = lax.axis_index("sess")
    my_x, my_y, my_z = lax.rem(me, side_x), lax.rem(lax.div(me, side_x), side_y), lax.div(me, side_x * side_y)

    xs = [lax.rem(my_x + d, side_x) for d in range(side_x)]
    ys = [lax.rem(my_y + d, side_y) * side_x for d in range(side_y)]
    zs = [lax.rem(my_z + d, side_z) * (side_x * side_y) for d in range(side_z)]
    order = far_first(side_x, side_y, side_z)
    peers = [zs[c] + ys[b] + xs[a] for a, b, c in order]
    origins = [zs[-c] + ys[-b] + xs[-a] for a, b, c in order]

    def block_rows(j):
        return pl.ds(pl.multiple_of(j * BLK, BLK), BLK)

    def load(which, hbm, buffer, j):
        return pltpu.make_async_copy(hbm.at[block_rows(j)], buffer.at[block_rows(j)], load_sem.at[which, j])

    small = [
        pltpu.make_async_copy(a, b, step_sem.at[i])
        for i, (a, b) in enumerate(((sq_hbm, sq), (rates_hbm, rates_ref), (step_rates_hbm, step_rates_ref), (sk_hbm, sk), (sv_hbm, sv)))
    ]
    for copy in small[:3]:
        copy.start()
    for j in range(blocks):
        load(0, k_hbm, kb, j).start()
        load(1, v_hbm, vb, j).start()
    for copy in small[3:]:
        copy.start()
    for j in range(blocks):
        load(2, q_hbm, qb, j).start()

    barrier = pltpu.get_barrier_semaphore()
    pl.semaphore_signal(barrier, inc=1, device_id=(1 - core, me), device_id_type=MESH)

    for other in peers:
        pl.semaphore_signal(barrier, inc=1, device_id=(core, other), device_id_type=MESH)

    small[0].wait()

    def fill(s, carry):
        row = place_ref[s]
        slots[s] = jnp.where(row < rows_here, sq[jnp.minimum(row, rows_here - 1)], jnp.zeros(sq.shape[1:], BF16))
        return carry

    lax.fori_loop(0, sessions, fill, 0)
    arrived[sessions - 1] = slots[me]

    pl.semaphore_wait(barrier, sessions)

    count_a = sessions // 2
    peer_spans = ((0, count_a), (count_a, sessions - 1))

    def dispatch(n):
        group = int(n >= count_a)
        return pltpu.make_async_remote_copy(
            src_ref=slots.at[peers[n]], dst_ref=arrived.at[n], send_sem=send_sem.at[group], recv_sem=recv_sem.at[group],
            device_id=(core, peers[n]), device_id_type=MESH)

    def give_back(n):
        return pltpu.make_async_remote_copy(
            src_ref=projected.at[n], dst_ref=back.at[me], send_sem=send_sem.at[2], recv_sem=recv_sem.at[2],
            device_id=(core, origins[n]), device_id_type=MESH)

    def wait_all(src, dst, span, n):
        part = pl.ds(span[0], span[1] - span[0])
        whole = pltpu.make_async_remote_copy(
            src_ref=src.at[part], dst_ref=dst.at[part], send_sem=send_sem.at[n],
            recv_sem=recv_sem.at[n], device_id=(core, peers[0]), device_id_type=MESH)
        whole.wait()

    for n in range(sessions - 1):
        dispatch(n).start()

    for copy in small[1:3]:
        copy.wait()
    lives = [(core * blocks + j < valid_ref[0]).astype(F32) for j in range(blocks)]
    masked = jnp.concatenate([rates_ref[:, j * BLK:(j + 1) * BLK] * lives[j] for j in range(blocks)], axis=0)
    upper = (iota((BLK, BLK), 0) <= iota((BLK, BLK), 1)).astype(F32).astype(BF16)
    summed = dot(jnp.concatenate(split3(masked), axis=0), upper)
    count = blocks * heads
    running_all = summed[:count] + summed[count:2 * count] + summed[2 * count:]
    lane = iota((heads, BLK), 1)
    passed = jnp.zeros((heads, 1), F32)
    for j in range(blocks):
        running = running_all[j * heads:(j + 1) * heads]
        last = running[:, BLK - 1:BLK]
        key_gain[j] = jnp.exp(running - last) * lives[j]
        block_gain[j] = jnp.broadcast_to(jnp.exp(-last), (heads, DH))
        entry_gain[j] = jnp.broadcast_to(jnp.exp(-passed), (heads, DH))
        passed = passed + last
        centre = None
        for b in range(subs):
            middle = running[:, b * SUB + SUB // 2:b * SUB + SUB // 2 + 1]
            doublings = jnp.round(middle * (1.0 / LN2))
            level = doublings * LN2
            row_gain[j, b] = jnp.exp(running - level)
            query_gain[j, b] = jnp.broadcast_to(jnp.exp2(-doublings), (heads, DH)).astype(BF16).astype(F32)
            centre = level if b == 0 else jnp.where(lane >= b * SUB, level, centre)
        low = (DH * EPSILON) * jnp.exp(2.0 * (running - centre))
        floor[j] = jnp.concatenate([low, jnp.zeros((DH - heads, BLK), F32)], axis=0).T
    for h in range(heads):
        decays[h] = jnp.broadcast_to(entry_gain[blocks - 1, h:h + 1, :] * block_gain[blocks - 1, h:h + 1, :], (8, DH))
    states[0] = jnp.zeros(states.shape[1:], F32)

    per_step = [step_rates_ref[i].astype(F32) for i in range(steps)]
    spans = []
    for delta in range(1, steps + 1):
        spans.append([sum(per_step[max(0, i - delta + 1):i + 1]) for i in range(steps)])
    tables = [
        jnp.concatenate([jnp.exp(-spans[delta - 1][i]) if i >= delta else jnp.zeros_like(per_step[0]) for i in range(steps)], axis=0)
        for delta in range(1, steps)
    ]
    tables.append(jnp.concatenate([jnp.exp(-spans[i][i]) for i in range(steps)], axis=0))
    flat = share * steps
    line = iota((flat, 2 * flat), 0)
    column = lax.rem(iota((flat, 2 * flat), 1), flat)
    pick = (column == lax.rem(line, steps) * share + lax.div(line, steps)).astype(F32).astype(BF16)
    for n, table in enumerate(tables):
        top = table.astype(BF16)
        rest = (table - top.astype(F32)).astype(BF16)
        gain_table[n] = dot(pick, jnp.concatenate([top, rest], axis=0))

    def group_cols(g):
        return pl.ds(pl.multiple_of(g * 4 * DH, 4 * DH), 4 * DH)

    def state_lap(j, g):
        rows, cols = block_rows(j), group_cols(g)
        keys, values = kb[rows, cols], vb[rows, cols]
        for one in range(4):
            h = g * 4 + one
            lanes = slice(one * DH, (one + 1) * DH)
            weighted = (keys[:, lanes].T.astype(F32) * key_gain[j, pl.ds(h, 1), :]).astype(BF16)
            states[j + 1, h] = block_gain[j, pl.ds(h, 1), :] * states[j, h] + dot(weighted, values[:, lanes])

    def state_block(j, carry):
        load(0, k_hbm, kb, j).wait()
        load(1, v_hbm, vb, j).wait()

        def state_group(g, carry):
            state_lap(j, g)
            return carry

        return lax.fori_loop(0, groups, state_group, carry)

    decay_copy = pltpu.make_async_remote_copy(
        src_ref=decays, dst_ref=other_decays, send_sem=pair_send_sem.at[2], recv_sem=pair_recv_sem.at[2],
        device_id=(1 - core, me), device_id_type=MESH)
    decay_copy.start()
    lax.fori_loop(0, blocks - 1, state_block, 0)

    load(0, k_hbm, kb, blocks - 1).wait()
    load(1, v_hbm, vb, blocks - 1).wait()

    def send_states(first, n, which):
        some = pl.ds(first, n)
        return pltpu.make_async_remote_copy(
            src_ref=states.at[blocks, some], dst_ref=other_states.at[some], send_sem=pair_send_sem.at[which],
            recv_sem=pair_recv_sem.at[which], device_id=(1 - core, me), device_id_type=MESH)

    for which in range(2):
        first = (1 - core if which == 0 else core) * (groups // 2)

        def last_group(g, carry):
            state_lap(blocks - 1, first + g)
            send_states((first + g) * 4, 4, which).start()
            return carry

        lax.fori_loop(0, groups // 2, last_group, 0)

    for copy in small[3:]:
        copy.wait()
    part = 4 * flat

    def part_rows(p):
        return pl.ds(pl.multiple_of(p * part, part), part)

    def recent_part(p, carry):
        q, k, v = (ref[pl.ds(p * 4, 4)].reshape(part, DH).astype(F32) for ref in (sq, sk, sv))
        own = iota((part, rows_here), 1) == lax.div(iota((part, rows_here), 0), flat) + p * 4

        def gain(n):
            tiled = jnp.concatenate([gain_table[n]] * 4, axis=0)
            return jnp.sum(jnp.where(own, tiled, 0.0), axis=1, keepdims=True)

        total = jnp.sum(q * k, axis=1, keepdims=True) * v
        for delta in range(1, steps):
            affinity = jnp.sum(q * pltpu.roll(k, delta, 0), axis=1, keepdims=True)
            total = total + (affinity * gain(delta - 1)) * pltpu.roll(v, delta, 0)
        recent[part_rows(p), :] = total
        carry_gain[part_rows(p), :] = jnp.broadcast_to(gain(steps - 1), (part, DH))
        return carry

    lax.fori_loop(0, rows_here // 4, recent_part, 0)

    half = BLK // 2
    first_core = core == 0
    per_half = half // SUB

    laps = blocks * groups
    live = [(core * blocks + j < valid_ref[0]).astype(F32) * math.sqrt(DH) for j in range(blocks)]

    def place_of(lap):
        lap = jnp.clip(lap, 0, laps - 1)
        return lax.div(lap, groups), lax.rem(lap, groups)

    def start_scores(lap):
        j, g = place_of(lap)
        rows, cols = block_rows(j), group_cols(g)
        q4, k4 = qb[rows, cols], kb[rows, cols]
        for one in range(4):
            h = g * 4 + one
            lanes = slice(one * DH, (one + 1) * DH)
            q, k = q4[:, lanes], k4[:, lanes]
            for side in range(2):
                here = slice(side * half, (side + 1) * half)
                seen = (side + 1) * half
                scores = dot(q[here], k[:seen], ((1,), (1,)))
                pieces = []
                for b in range(per_half):
                    n = side * per_half + b
                    piece = scores[b * SUB:(b + 1) * SUB] * row_gain[j, n, pl.ds(h, 1), :][:, :seen]
                    causal = iota((SUB, half), 0) + b * SUB >= iota((SUB, half), 1)
                    latest = jnp.where(causal, piece[:, seen - half:], 0.0)
                    scaled = q[here][b * SUB:(b + 1) * SUB].astype(F32) * query_gain[j, n, pl.ds(h, 1), :]
                    pieces.append(jnp.concatenate(([piece[:, :half]] if side else []) + [latest, scaled], axis=1).astype(BF16))
                mixed[one, :, side * 2 * half:side * 2 * half + seen + half] = jnp.concatenate(pieces, axis=0)

    def apply_values(lap):
        j, g = place_of(lap)
        v4 = vb[block_rows(j), group_cols(g)]
        for one in range(4):
            h = g * 4 + one
            v = v4[:, one * DH:(one + 1) * DH]
            prefix = jnp.where(first_core, 0.0, entry_gain[j, pl.ds(h, 1), :] * other_states[h])
            entering = (prefix + states[j, h]).astype(BF16)
            for side in range(2):
                seen = (side + 1) * half
                weights = mixed[one, :, side * 2 * half:side * 2 * half + seen + half]
                raw[one, side * half:(side + 1) * half, :] = dot(weights, jnp.concatenate([v[:seen], entering], axis=0))

    def normalize(lap):
        j, g = place_of(lap)
        alive = jnp.where(j == 0, live[0], live[1])
        for n in range(2, blocks):
            alive = jnp.where(j == n, live[n], alive)
        for one in range(4):
            h = g * 4 + one
            for side in range(2):
                here = slice(side * half, (side + 1) * half)
                mix = raw[one, here, :]
                low = jnp.where(iota((half, DH), 1) == h, floor[j, here, :], 0.0)
                scale = lax.rsqrt(jnp.sum(mix * mix + low, axis=1, keepdims=True)) * alive
                out_ref[pl.ds(pl.multiple_of(j * BLK + side * half, half), half), pl.ds(pl.multiple_of(h * DH, DH), DH)] = (
                    mix * scale).astype(BF16)

    def output_lap(lap, carry):
        normalize(lap - 2)
        apply_values(lap - 1)
        start_scores(lap)
        return carry

    def project_group(low, high):
        many = high - low

        def project(quad, carry):
            place = pl.ds(pl.multiple_of(quad * 16, 16), 16)
            x = arrived[low:high, place, :].reshape(many * 16, DH)
            doubled = jnp.concatenate([x, x], axis=1)
            position = lax.div(iota((1, 16, DH), 1), 4)
            chosen = None
            for two in range(2):
                columns = []
                for one in range(2):
                    h = core * share + quad * 4 + two * 2 + one
                    mine, other = states[blocks, h], other_states[h]
                    earlier = jnp.where(first_core, mine, other)
                    latter = jnp.where(first_core, other, mine)
                    decay = jnp.where(first_core, other_decays[h, 0:1, :], decays[h, 0:1, :])
                    final = decay * earlier + latter
                    top = final.astype(BF16)
                    rest = (final - top.astype(F32)).astype(BF16)
                    columns.append(jnp.concatenate([top, rest], axis=0))
                product = dot(doubled, jnp.concatenate(columns, axis=1))
                for one in range(2):
                    piece = product[:, one * DH:(one + 1) * DH].reshape(many, 16, DH)
                    chosen = piece if chosen is None else jnp.where(position == two * 2 + one, piece, chosen)
            projected[low:high, place, :] = chosen.astype(BF16)
            return carry

        lax.fori_loop(0, share // 4, project, 0)

    raw[...] = jnp.zeros(raw.shape, F32)
    mixed[...] = jnp.zeros(mixed.shape, BF16)
    decay_copy.wait()
    send_states(pl.multiple_of(core * share, share), share, 0).wait()
    wait_all(slots, arrived, peer_spans[0], 0)
    project_group(0, count_a)
    for n in range(count_a):
        give_back(n).start()

    for j in range(blocks):
        load(2, q_hbm, qb, j).wait()
    send_states(pl.multiple_of((1 - core) * share, share), share, 1).wait()
    lax.fori_loop(0, EARLY, output_lap, 0)

    wait_all(slots, arrived, peer_spans[1], 1)
    project_group(count_a, sessions)
    back[me] = projected[sessions - 1]
    for n in range(count_a, sessions - 1):
        give_back(n).start()

    lax.fori_loop(EARLY, laps + 2, output_lap, 0)

    wait_all(projected, back, (0, sessions - 1), 2)

    def finish(p, carry):
        rows = part_rows(p)
        pieces = [back[session_ref[p * 4 + i]].astype(F32) for i in range(4)]
        reading = carry_gain[rows, :] * jnp.concatenate(pieces, axis=0) + recent[rows, :]
        scale = lax.rsqrt(jnp.mean(reading * reading, axis=1, keepdims=True) + EPSILON)
        decoded_ref[rows, :] = (reading * scale).astype(BF16)
        return carry

    lax.fori_loop(0, rows_here // 4, finish, 0)


def local(side, query_rows, key_rows, value_rows, decay_rates, valid_blocks, step_queries, step_keys, step_values, step_rates, row_session):
    tokens, width = query_rows.shape[1:]
    heads = decay_rates.shape[2]
    blocks = tokens // BLK
    subs = BLK // SUB
    row_count, steps, share_width = step_queries.shape
    share = share_width // DH
    sessions = lax.axis_size("sess")

    def by_head(data):
        return data.reshape(row_count, steps, share, DH).transpose(0, 2, 1, 3).reshape(row_count, share * steps, DH)

    named = row_session[:, 0][None, :] == jnp.arange(sessions, dtype=jnp.int32)[:, None]
    place = jnp.min(jnp.where(named, jnp.arange(row_count, dtype=jnp.int32)[None, :], row_count), axis=1)
    flat_rows = row_count * share * steps

    smem = pl.BlockSpec(memory_space=pltpu.SMEM)
    vmem = pl.BlockSpec(memory_space=pltpu.VMEM)
    hbm = pl.BlockSpec(memory_space=pl.ANY)
    slot = (share * steps, DH)
    dma = pltpu.SemaphoreType.DMA
    prefill_out, decoded = pl.pallas_call(
        functools.partial(fused_kernel, (heads, blocks, sessions, row_count, steps, side)),
        out_shape=(pltpu.VMEM((tokens, width), BF16), pltpu.VMEM((flat_rows, DH), BF16)),
        in_specs=[smem, smem, smem] + [hbm] * 8,
        out_specs=(vmem, vmem),
        scratch_shapes=[
            pltpu.VMEM((tokens, width), BF16), pltpu.VMEM((tokens, width), BF16), pltpu.VMEM((tokens, width), BF16),
            pltpu.VMEM((heads, tokens), F32), pltpu.VMEM((steps, share, row_count), BF16),
            pltpu.VMEM((row_count,) + slot, BF16), pltpu.VMEM((row_count,) + slot, BF16), pltpu.VMEM((row_count,) + slot, BF16),
            pltpu.VMEM((sessions,) + slot, BF16), pltpu.VMEM((sessions,) + slot, BF16),
            pltpu.VMEM((sessions,) + slot, BF16), pltpu.VMEM((sessions,) + slot, BF16),
            pltpu.VMEM((flat_rows, DH), F32), pltpu.VMEM((flat_rows, DH), F32), pltpu.VMEM((steps, share * steps, row_count), F32),
            pltpu.VMEM((blocks + 1, heads, DH, DH), F32), pltpu.VMEM((heads, DH, DH), F32),
            pltpu.VMEM((heads, 8, DH), F32), pltpu.VMEM((heads, 8, DH), F32),
            pltpu.VMEM((blocks, heads, BLK), F32), pltpu.VMEM((blocks, heads, DH), F32), pltpu.VMEM((blocks, heads, DH), F32),
            pltpu.VMEM((blocks, subs, heads, BLK), F32), pltpu.VMEM((blocks, subs, heads, DH), F32),
            pltpu.VMEM((blocks, BLK, DH), F32), pltpu.VMEM((4, BLK // 2, 5 * BLK // 2), BF16), pltpu.VMEM((4, BLK, DH), F32),
            dma((3, blocks)), dma((5,)), dma((3,)), dma((3,)), dma((3,)), dma((3,)),
        ],
        compiler_params=pltpu.CompilerParams(collective_id=0, has_side_effects=True, vmem_limit_bytes=48 << 20),
    )(valid_blocks, place, row_session[:, 0], decay_rates[0].T, step_rates.transpose(1, 2, 0), query_rows[0], key_rows[0], value_rows[0],
      by_head(step_queries), by_head(step_keys), by_head(step_values))
    decode_out = decoded.reshape(row_count, share, steps, DH).transpose(0, 2, 1, 3).reshape(row_count, steps, share_width)
    return prefill_out[None], decode_out


def solution(mesh):
    long, step = P("sess", "ctx", None), P("sess", None, "ctx")
    devices = mesh.shape["sess"]
    side = round(devices ** (1 / 3))
    sides = (side, side, side) if side ** 3 == devices else (1, 1, devices)
    return jax.shard_map(
        functools.partial(local, sides),
        mesh=mesh,
        in_specs=(long, long, long, long, P("sess"), step, step, step, step, P("sess", None)),
        out_specs=(long, step),
        check_vma=False,
    )
```

```python
import functools
import math

import jax
import jax.numpy as jnp
from jax import lax
from jax.experimental import pallas as pl
from jax.experimental.pallas import tpu as pltpu
from jax.sharding import PartitionSpec as P

BLK = 256
DH = 128
SUB = 64
EPSILON = 1e-06
F32 = jnp.float32
BF16 = jnp.bfloat16
MESH = pl.DeviceIdType.MESH
LN2 = math.log(2.0)
EARLY = 3


def dot(a, b, dims=((1,), (0,))):
    return lax.dot_general(a, b, (dims, ((), ())), preferred_element_type=F32)


def iota(shape, axis):
    return lax.broadcasted_iota(jnp.int32, shape, axis)


def split3(value):
    first = value.astype(BF16)
    second = (value - first.astype(F32)).astype(BF16)
    third = (value - first.astype(F32) - second.astype(F32)).astype(BF16)
    return first, second, third


def far_first(side_x, side_y, side_z):
    sides = (side_x, side_y, side_z)

    def hops(offset):
        return sum(min(d, n - d) for d, n in zip(offset, sides))

    def orbit(offset):
        turned = [offset]
        if side_x == side_y == side_z:
            turned += [offset[1:] + offset[:1], offset[2:] + offset[:2]]
        for one in turned:
            yield one
            yield tuple((n - d) % n for d, n in zip(one, sides))

    every = [(a, b, c) for a in range(side_x) for b in range(side_y) for c in range(side_z)][1:]
    order = []
    for offset in sorted(every, key=lambda o: (-hops(o), o)):
        for one in orbit(offset):
            if one not in order:
                order.append(one)
    return order


def fused_kernel(
    sizes,
    valid_ref, place_ref, session_ref, rates_hbm, step_rates_hbm, q_hbm, k_hbm, v_hbm, sq_hbm, sk_hbm, sv_hbm,
    out_ref, decoded_ref,
    qb, kb, vb, rates_ref, step_rates_ref, sq, sk, sv, slots, arrived, projected, back, recent, carry_gain, gain_table,
    states, other_states, decays, other_decays,
    key_gain, block_gain, entry_gain, row_gain, query_gain, floor, mixed,
    load_sem, step_sem, send_sem, recv_sem, pair_send_sem, pair_recv_sem,
):
    heads, blocks, sessions, rows_here, steps, (side_z, side_y, side_x) = sizes
    share = heads // 2
    groups = heads // 4
    subs = BLK // SUB
    core = lax.axis_index("ctx")
    me = lax.axis_index("sess")
    my_x, my_y, my_z = lax.rem(me, side_x), lax.rem(lax.div(me, side_x), side_y), lax.div(me, side_x * side_y)

    xs = [lax.rem(my_x + d, side_x) for d in range(side_x)]
    ys = [lax.rem(my_y + d, side_y) * side_x for d in range(side_y)]
    zs = [lax.rem(my_z + d, side_z) * (side_x * side_y) for d in range(side_z)]
    order = far_first(side_x, side_y, side_z)
    peers = [zs[c] + ys[b] + xs[a] for a, b, c in order]
    origins = [zs[-c] + ys[-b] + xs[-a] for a, b, c in order]

    def block_rows(j):
        return pl.ds(pl.multiple_of(j * BLK, BLK), BLK)

    def load(which, hbm, buffer, j):
        return pltpu.make_async_copy(hbm.at[block_rows(j)], buffer.at[block_rows(j)], load_sem.at[which, j])

    small = [
        pltpu.make_async_copy(a, b, step_sem.at[i])
        for i, (a, b) in enumerate(((sq_hbm, sq), (rates_hbm, rates_ref), (step_rates_hbm, step_rates_ref), (sk_hbm, sk), (sv_hbm, sv)))
    ]
    for copy in small[:3]:
        copy.start()
    for j in range(blocks):
        load(0, k_hbm, kb, j).start()
        load(1, v_hbm, vb, j).start()
    for copy in small[3:]:
        copy.start()
    for j in range(blocks):
        load(2, q_hbm, qb, j).start()

    barrier = pltpu.get_barrier_semaphore()
    pl.semaphore_signal(barrier, inc=1, device_id=(1 - core, me), device_id_type=MESH)

    for other in peers:
        pl.semaphore_signal(barrier, inc=1, device_id=(core, other), device_id_type=MESH)

    small[0].wait()

    def fill(n, carry):
        for one in range(8):
            row = place_ref[n * 8 + one]
            slots[n * 8 + one] = jnp.where(row < rows_here, sq[jnp.minimum(row, rows_here - 1)], jnp.zeros(sq.shape[1:], BF16))
        return carry

    lax.fori_loop(0, sessions // 8, fill, 0)
    arrived[sessions - 1] = slots[me]

    pl.semaphore_wait(barrier, sessions)

    count_a = sessions // 2
    peer_spans = ((0, count_a), (count_a, sessions - 1))

    def dispatch(n):
        group = int(n >= count_a)
        return pltpu.make_async_remote_copy(
            src_ref=slots.at[peers[n]], dst_ref=arrived.at[n], send_sem=send_sem.at[group], recv_sem=recv_sem.at[group],
            device_id=(core, peers[n]), device_id_type=MESH)

    def give_back(n):
        return pltpu.make_async_remote_copy(
            src_ref=projected.at[n], dst_ref=back.at[me], send_sem=send_sem.at[2], recv_sem=recv_sem.at[2],
            device_id=(core, origins[n]), device_id_type=MESH)

    def wait_all(src, dst, span, n):
        part = pl.ds(span[0], span[1] - span[0])
        whole = pltpu.make_async_remote_copy(
            src_ref=src.at[part], dst_ref=dst.at[part], send_sem=send_sem.at[n],
            recv_sem=recv_sem.at[n], device_id=(core, peers[0]), device_id_type=MESH)
        whole.wait()

    for n in range(sessions - 1):
        dispatch(n).start()

    for copy in small[1:3]:
        copy.wait()
    lives = [(core * blocks + j < valid_ref[0]).astype(F32) for j in range(blocks)]
    masked = jnp.concatenate([rates_ref[:, j * BLK:(j + 1) * BLK] * lives[j] for j in range(blocks)], axis=0)
    upper = (iota((BLK, BLK), 0) <= iota((BLK, BLK), 1)).astype(F32).astype(BF16)
    summed = dot(jnp.concatenate(split3(masked), axis=0), upper)
    count = blocks * heads
    running_all = summed[:count] + summed[count:2 * count] + summed[2 * count:]
    lane = iota((heads, BLK), 1)
    passed = jnp.zeros((heads, 1), F32)
    for j in range(blocks):
        running = running_all[j * heads:(j + 1) * heads]
        last = running[:, BLK - 1:BLK]
        key_gain[j] = jnp.exp(running - last) * lives[j]
        block_gain[j] = jnp.broadcast_to(jnp.exp(-last), (heads, DH))
        entry_gain[j] = jnp.broadcast_to(jnp.exp(-passed), (heads, DH))
        passed = passed + last
        centre = None
        for b in range(subs):
            middle = running[:, b * SUB + SUB // 2:b * SUB + SUB // 2 + 1]
            doublings = jnp.round(middle * (1.0 / LN2))
            level = doublings * LN2
            row_gain[j, b] = jnp.exp(running - level)
            query_gain[j, b] = jnp.broadcast_to(jnp.exp2(-doublings), (heads, DH)).astype(BF16).astype(F32)
            centre = level if b == 0 else jnp.where(lane >= b * SUB, level, centre)
        low = (DH * EPSILON) * jnp.exp(2.0 * (running - centre))
        floor[j] = jnp.concatenate([low, jnp.zeros((DH - heads, BLK), F32)], axis=0).T
    for h in range(heads):
        decays[h] = jnp.broadcast_to(entry_gain[blocks - 1, h:h + 1, :] * block_gain[blocks - 1, h:h + 1, :], (8, DH))
    states[0] = jnp.zeros(states.shape[1:], F32)

    per_step = [step_rates_ref[i].astype(F32) for i in range(steps)]
    spans = []
    for delta in range(1, steps + 1):
        spans.append([sum(per_step[max(0, i - delta + 1):i + 1]) for i in range(steps)])
    tables = [
        jnp.concatenate([jnp.exp(-spans[delta - 1][i]) if i >= delta else jnp.zeros_like(per_step[0]) for i in range(steps)], axis=0)
        for delta in range(1, steps)
    ]
    tables.append(jnp.concatenate([jnp.exp(-spans[i][i]) for i in range(steps)], axis=0))
    flat = share * steps
    line = iota((flat, 2 * flat), 0)
    column = lax.rem(iota((flat, 2 * flat), 1), flat)
    pick = (column == lax.rem(line, steps) * share + lax.div(line, steps)).astype(F32).astype(BF16)
    for n, table in enumerate(tables):
        top = table.astype(BF16)
        rest = (table - top.astype(F32)).astype(BF16)
        gain_table[n] = dot(pick, jnp.concatenate([top, rest], axis=0))

    def group_cols(g):
        return pl.ds(pl.multiple_of(g * 4 * DH, 4 * DH), 4 * DH)

    def state_lap(j, g):
        rows, cols = block_rows(j), group_cols(g)
        keys, values = kb[rows, cols], vb[rows, cols]
        for one in range(4):
            h = g * 4 + one
            lanes = slice(one * DH, (one + 1) * DH)
            weighted = (keys[:, lanes].T.astype(F32) * key_gain[j, pl.ds(h, 1), :]).astype(BF16)
            states[j + 1, h] = block_gain[j, pl.ds(h, 1), :] * states[j, h] + dot(weighted, values[:, lanes])

    def state_block(j, carry):
        load(0, k_hbm, kb, j).wait()
        load(1, v_hbm, vb, j).wait()

        def state_group(g, carry):
            state_lap(j, g)
            return carry

        return lax.fori_loop(0, groups, state_group, carry)

    decay_copy = pltpu.make_async_remote_copy(
        src_ref=decays, dst_ref=other_decays, send_sem=pair_send_sem.at[2], recv_sem=pair_recv_sem.at[2],
        device_id=(1 - core, me), device_id_type=MESH)
    decay_copy.start()
    lax.fori_loop(0, blocks - 1, state_block, 0)

    load(0, k_hbm, kb, blocks - 1).wait()
    load(1, v_hbm, vb, blocks - 1).wait()

    def send_states(first, n, which):
        some = pl.ds(first, n)
        return pltpu.make_async_remote_copy(
            src_ref=states.at[blocks, some], dst_ref=other_states.at[some], send_sem=pair_send_sem.at[which],
            recv_sem=pair_recv_sem.at[which], device_id=(1 - core, me), device_id_type=MESH)

    for which in range(2):
        first = (1 - core if which == 0 else core) * (groups // 2)

        def last_group(g, carry):
            state_lap(blocks - 1, first + g)
            send_states((first + g) * 4, 4, which).start()
            return carry

        lax.fori_loop(0, groups // 2, last_group, 0)

    for copy in small[3:]:
        copy.wait()
    part = 4 * flat

    def part_rows(p):
        return pl.ds(pl.multiple_of(p * part, part), part)

    def recent_part(p, carry):
        q, k, v = (ref[pl.ds(p * 4, 4)].reshape(part, DH).astype(F32) for ref in (sq, sk, sv))
        own = iota((part, rows_here), 1) == lax.div(iota((part, rows_here), 0), flat) + p * 4

        def gain(n):
            tiled = jnp.concatenate([gain_table[n]] * 4, axis=0)
            return jnp.sum(jnp.where(own, tiled, 0.0), axis=1, keepdims=True)

        total = jnp.sum(q * k, axis=1, keepdims=True) * v
        for delta in range(1, steps):
            affinity = jnp.sum(q * pltpu.roll(k, delta, 0), axis=1, keepdims=True)
            total = total + (affinity * gain(delta - 1)) * pltpu.roll(v, delta, 0)
        recent[part_rows(p), :] = total
        carry_gain[part_rows(p), :] = jnp.broadcast_to(gain(steps - 1), (part, DH))
        return carry

    lax.fori_loop(0, rows_here // 4, recent_part, 0)

    half = BLK // 2
    first_core = core == 0
    per_half = half // SUB

    laps = blocks * groups
    live = [(core * blocks + j < valid_ref[0]).astype(F32) * math.sqrt(DH) for j in range(blocks)]

    def place_of(lap):
        lap = jnp.clip(lap, 0, laps - 1)
        return lax.div(lap, groups), lax.rem(lap, groups)

    def start_scores(lap):
        j, g = place_of(lap)
        rows, cols = block_rows(j), group_cols(g)
        q4, k4 = qb[rows, cols], kb[rows, cols]
        for one in range(4):
            h = g * 4 + one
            lanes = slice(one * DH, (one + 1) * DH)
            q, k = q4[:, lanes], k4[:, lanes]
            for side in range(2):
                here = slice(side * half, (side + 1) * half)
                seen = (side + 1) * half
                scores = dot(q[here], k[:seen], ((1,), (1,)))
                pieces = []
                for b in range(per_half):
                    n = side * per_half + b
                    piece = scores[b * SUB:(b + 1) * SUB] * row_gain[j, n, pl.ds(h, 1), :][:, :seen]
                    causal = iota((SUB, half), 0) + b * SUB >= iota((SUB, half), 1)
                    latest = jnp.where(causal, piece[:, seen - half:], 0.0)
                    scaled = q[here][b * SUB:(b + 1) * SUB].astype(F32) * query_gain[j, n, pl.ds(h, 1), :]
                    pieces.append(jnp.concatenate(([piece[:, :half]] if side else []) + [latest, scaled], axis=1).astype(BF16))
                mixed[one, :, side * 2 * half:side * 2 * half + seen + half] = jnp.concatenate(pieces, axis=0)

    def apply_values(lap):
        j, g = place_of(lap)
        alive = jnp.where(j == 0, live[0], live[1])
        for n in range(2, blocks):
            alive = jnp.where(j == n, live[n], alive)
        v4 = vb[block_rows(j), group_cols(g)]
        for one in range(4):
            h = g * 4 + one
            v = v4[:, one * DH:(one + 1) * DH]
            prefix = jnp.where(first_core, 0.0, entry_gain[j, pl.ds(h, 1), :] * other_states[h])
            entering = (prefix + states[j, h]).astype(BF16)
            for side in range(2):
                here = slice(side * half, (side + 1) * half)
                seen = (side + 1) * half
                weights = mixed[one, :, side * 2 * half:side * 2 * half + seen + half]
                mix = dot(weights, jnp.concatenate([v[:seen], entering], axis=0))
                low = jnp.where(iota((half, DH), 1) == h, floor[j, here, :], 0.0)
                scale = lax.rsqrt(jnp.sum(mix * mix + low, axis=1, keepdims=True)) * alive
                out_ref[pl.ds(pl.multiple_of(j * BLK + side * half, half), half), pl.ds(pl.multiple_of(h * DH, DH), DH)] = (
                    mix * scale).astype(BF16)

    def output_lap(lap, carry):
        apply_values(lap - 1)
        start_scores(lap)
        return carry

    def project_group(low, high):
        many = high - low

        def project(quad, carry):
            place = pl.ds(pl.multiple_of(quad * 16, 16), 16)
            x = arrived[low:high, place, :].reshape(many * 16, DH)
            doubled = jnp.concatenate([x, x], axis=1)
            position = lax.div(iota((1, 16, DH), 1), 4)
            chosen = None
            for two in range(2):
                columns = []
                for one in range(2):
                    h = core * share + quad * 4 + two * 2 + one
                    mine, other = states[blocks, h], other_states[h]
                    earlier = jnp.where(first_core, mine, other)
                    latter = jnp.where(first_core, other, mine)
                    decay = jnp.where(first_core, other_decays[h, 0:1, :], decays[h, 0:1, :])
                    final = decay * earlier + latter
                    top = final.astype(BF16)
                    rest = (final - top.astype(F32)).astype(BF16)
                    columns.append(jnp.concatenate([top, rest], axis=0))
                product = dot(doubled, jnp.concatenate(columns, axis=1))
                for one in range(2):
                    piece = product[:, one * DH:(one + 1) * DH].reshape(many, 16, DH)
                    chosen = piece if chosen is None else jnp.where(position == two * 2 + one, piece, chosen)
            projected[low:high, place, :] = chosen.astype(BF16)
            return carry

        lax.fori_loop(0, share // 4, project, 0)

    mixed[...] = jnp.zeros(mixed.shape, BF16)
    decay_copy.wait()
    send_states(pl.multiple_of(core * share, share), share, 0).wait()
    wait_all(slots, arrived, peer_spans[0], 0)
    project_group(0, count_a)
    for n in range(count_a):
        give_back(n).start()

    for j in range(blocks):
        load(2, q_hbm, qb, j).wait()
    send_states(pl.multiple_of((1 - core) * share, share), share, 1).wait()
    lax.fori_loop(0, EARLY, output_lap, 0)

    wait_all(slots, arrived, peer_spans[1], 1)
    project_group(count_a, sessions)
    back[me] = projected[sessions - 1]
    for n in range(count_a, sessions - 1):
        give_back(n).start()

    lax.fori_loop(EARLY, laps + 1, output_lap, 0)

    wait_all(projected, back, (0, sessions - 1), 2)

    def finish_part(p):
        rows = part_rows(p)
        pieces = [back[session_ref[p * 4 + i]].astype(F32) for i in range(4)]
        reading = carry_gain[rows, :] * jnp.concatenate(pieces, axis=0) + recent[rows, :]
        scale = lax.rsqrt(jnp.mean(reading * reading, axis=1, keepdims=True) + EPSILON)
        decoded_ref[rows, :] = (reading * scale).astype(BF16)

    def finish(p, carry):
        finish_part(p * 2)
        finish_part(p * 2 + 1)
        return carry

    lax.fori_loop(0, rows_here // 8, finish, 0)


def local(side, query_rows, key_rows, value_rows, decay_rates, valid_blocks, step_queries, step_keys, step_values, step_rates, row_session):
    tokens, width = query_rows.shape[1:]
    heads = decay_rates.shape[2]
    blocks = tokens // BLK
    subs = BLK // SUB
    row_count, steps, share_width = step_queries.shape
    share = share_width // DH
    sessions = lax.axis_size("sess")

    def by_head(data):
        return data.reshape(row_count, steps, share, DH).transpose(0, 2, 1, 3).reshape(row_count, share * steps, DH)

    named = row_session[:, 0][None, :] == jnp.arange(sessions, dtype=jnp.int32)[:, None]
    place = jnp.min(jnp.where(named, jnp.arange(row_count, dtype=jnp.int32)[None, :], row_count), axis=1)
    flat_rows = row_count * share * steps

    smem = pl.BlockSpec(memory_space=pltpu.SMEM)
    vmem = pl.BlockSpec(memory_space=pltpu.VMEM)
    hbm = pl.BlockSpec(memory_space=pl.ANY)
    slot = (share * steps, DH)
    dma = pltpu.SemaphoreType.DMA
    prefill_out, decoded = pl.pallas_call(
        functools.partial(fused_kernel, (heads, blocks, sessions, row_count, steps, side)),
        out_shape=(pltpu.VMEM((tokens, width), BF16), pltpu.VMEM((flat_rows, DH), BF16)),
        in_specs=[smem, smem, smem] + [hbm] * 8,
        out_specs=(vmem, vmem),
        scratch_shapes=[
            pltpu.VMEM((tokens, width), BF16), pltpu.VMEM((tokens, width), BF16), pltpu.VMEM((tokens, width), BF16),
            pltpu.VMEM((heads, tokens), F32), pltpu.VMEM((steps, share, row_count), BF16),
            pltpu.VMEM((row_count,) + slot, BF16), pltpu.VMEM((row_count,) + slot, BF16), pltpu.VMEM((row_count,) + slot, BF16),
            pltpu.VMEM((sessions,) + slot, BF16), pltpu.VMEM((sessions,) + slot, BF16),
            pltpu.VMEM((sessions,) + slot, BF16), pltpu.VMEM((sessions,) + slot, BF16),
            pltpu.VMEM((flat_rows, DH), F32), pltpu.VMEM((flat_rows, DH), F32), pltpu.VMEM((steps, share * steps, row_count), F32),
            pltpu.VMEM((blocks + 1, heads, DH, DH), F32), pltpu.VMEM((heads, DH, DH), F32),
            pltpu.VMEM((heads, 8, DH), F32), pltpu.VMEM((heads, 8, DH), F32),
            pltpu.VMEM((blocks, heads, BLK), F32), pltpu.VMEM((blocks, heads, DH), F32), pltpu.VMEM((blocks, heads, DH), F32),
            pltpu.VMEM((blocks, subs, heads, BLK), F32), pltpu.VMEM((blocks, subs, heads, DH), F32),
            pltpu.VMEM((blocks, BLK, DH), F32), pltpu.VMEM((4, BLK // 2, 5 * BLK // 2), BF16),
            dma((3, blocks)), dma((5,)), dma((3,)), dma((3,)), dma((3,)), dma((3,)),
        ],
        compiler_params=pltpu.CompilerParams(collective_id=0, has_side_effects=True, vmem_limit_bytes=48 << 20),
    )(valid_blocks, place, row_session[:, 0], decay_rates[0].T, step_rates.transpose(1, 2, 0), query_rows[0], key_rows[0], value_rows[0],
      by_head(step_queries), by_head(step_keys), by_head(step_values))
    decode_out = decoded.reshape(row_count, share, steps, DH).transpose(0, 2, 1, 3).reshape(row_count, steps, share_width)
    return prefill_out[None], decode_out


def solution(mesh):
    long, step = P("sess", "ctx", None), P("sess", None, "ctx")
    devices = mesh.shape["sess"]
    side = round(devices ** (1 / 3))
    sides = (side, side, side) if side ** 3 == devices else (1, 1, devices)
    return jax.shard_map(
        functools.partial(local, sides),
        mesh=mesh,
        in_specs=(long, long, long, long, P("sess"), step, step, step, step, P("sess", None)),
        out_specs=(long, step),
        check_vma=False,
    )
```

```python
import functools
import math

import jax
import jax.numpy as jnp
from jax import lax
from jax.experimental import pallas as pl
from jax.experimental.pallas import tpu as pltpu
from jax.sharding import PartitionSpec as P

BLK = 256
DH = 128
SUB = 64
EPSILON = 1e-06
F32 = jnp.float32
BF16 = jnp.bfloat16
MESH = pl.DeviceIdType.MESH
LN2 = math.log(2.0)
EARLY = 2


def dot(a, b, dims=((1,), (0,))):
    return lax.dot_general(a, b, (dims, ((), ())), preferred_element_type=F32)


def iota(shape, axis):
    return lax.broadcasted_iota(jnp.int32, shape, axis)


def split3(value):
    first = value.astype(BF16)
    second = (value - first.astype(F32)).astype(BF16)
    third = (value - first.astype(F32) - second.astype(F32)).astype(BF16)
    return first, second, third


def far_first(side_x, side_y, side_z):
    sides = (side_x, side_y, side_z)

    def hops(offset):
        return sum(min(d, n - d) for d, n in zip(offset, sides))

    def orbit(offset):
        turned = [offset]
        if side_x == side_y == side_z:
            turned += [offset[1:] + offset[:1], offset[2:] + offset[:2]]
        for one in turned:
            yield one
            yield tuple((n - d) % n for d, n in zip(one, sides))

    every = [(a, b, c) for a in range(side_x) for b in range(side_y) for c in range(side_z)][1:]
    order = []
    for offset in sorted(every, key=lambda o: (-hops(o), o)):
        for one in orbit(offset):
            if one not in order:
                order.append(one)
    return order


def fused_kernel(
    sizes,
    valid_ref, place_ref, session_ref, rates_hbm, step_rates_hbm, q_hbm, k_hbm, v_hbm, sq_hbm, sk_hbm, sv_hbm,
    out_ref, decoded_ref,
    qb, kb, vb, rates_ref, step_rates_ref, sq, sk, sv, slots, arrived, projected, back, recent, carry_gain, gain_table,
    states, other_states, decays, other_decays,
    key_gain, block_gain, entry_gain, row_gain, query_gain, floor, mixed,
    load_sem, step_sem, send_sem, recv_sem, pair_send_sem, pair_recv_sem,
):
    heads, blocks, sessions, rows_here, steps, (side_z, side_y, side_x) = sizes
    share = heads // 2
    groups = heads // 4
    subs = BLK // SUB
    core = lax.axis_index("ctx")
    me = lax.axis_index("sess")
    my_x, my_y, my_z = lax.rem(me, side_x), lax.rem(lax.div(me, side_x), side_y), lax.div(me, side_x * side_y)

    xs = [lax.rem(my_x + d, side_x) for d in range(side_x)]
    ys = [lax.rem(my_y + d, side_y) * side_x for d in range(side_y)]
    zs = [lax.rem(my_z + d, side_z) * (side_x * side_y) for d in range(side_z)]
    order = far_first(side_x, side_y, side_z)
    peers = [zs[c] + ys[b] + xs[a] for a, b, c in order]
    origins = [zs[-c] + ys[-b] + xs[-a] for a, b, c in order]

    def block_rows(j):
        return pl.ds(pl.multiple_of(j * BLK, BLK), BLK)

    def load(which, hbm, buffer, j):
        return pltpu.make_async_copy(hbm.at[block_rows(j)], buffer.at[block_rows(j)], load_sem.at[which, j])

    small = [
        pltpu.make_async_copy(a, b, step_sem.at[i])
        for i, (a, b) in enumerate(((sq_hbm, sq), (rates_hbm, rates_ref), (step_rates_hbm, step_rates_ref), (sk_hbm, sk), (sv_hbm, sv)))
    ]
    for copy in small[:3]:
        copy.start()
    for j in range(blocks):
        load(0, k_hbm, kb, j).start()
        load(1, v_hbm, vb, j).start()
    for copy in small[3:]:
        copy.start()
    for j in range(blocks):
        load(2, q_hbm, qb, j).start()

    barrier = pltpu.get_barrier_semaphore()
    pl.semaphore_signal(barrier, inc=1, device_id=(1 - core, me), device_id_type=MESH)

    for other in peers:
        pl.semaphore_signal(barrier, inc=1, device_id=(core, other), device_id_type=MESH)

    small[0].wait()

    def fill(n, carry):
        for one in range(8):
            row = place_ref[n * 8 + one]
            slots[n * 8 + one] = jnp.where(row < rows_here, sq[jnp.minimum(row, rows_here - 1)], jnp.zeros(sq.shape[1:], BF16))
        return carry

    lax.fori_loop(0, sessions // 8, fill, 0)
    arrived[sessions - 1] = slots[me]

    pl.semaphore_wait(barrier, sessions)

    count_a = sessions // 2
    peer_spans = ((0, count_a), (count_a, sessions - 1))

    def dispatch(n):
        group = int(n >= count_a)
        return pltpu.make_async_remote_copy(
            src_ref=slots.at[peers[n]], dst_ref=arrived.at[n], send_sem=send_sem.at[group], recv_sem=recv_sem.at[group],
            device_id=(core, peers[n]), device_id_type=MESH)

    def give_back(n):
        return pltpu.make_async_remote_copy(
            src_ref=projected.at[n], dst_ref=back.at[me], send_sem=send_sem.at[2], recv_sem=recv_sem.at[2],
            device_id=(core, origins[n]), device_id_type=MESH)

    def wait_all(src, dst, span, n):
        part = pl.ds(span[0], span[1] - span[0])
        whole = pltpu.make_async_remote_copy(
            src_ref=src.at[part], dst_ref=dst.at[part], send_sem=send_sem.at[n],
            recv_sem=recv_sem.at[n], device_id=(core, peers[0]), device_id_type=MESH)
        whole.wait()

    for n in range(sessions - 1):
        dispatch(n).start()

    for copy in small[1:3]:
        copy.wait()
    lives = [(core * blocks + j < valid_ref[0]).astype(F32) for j in range(blocks)]
    masked = jnp.concatenate([rates_ref[:, j * BLK:(j + 1) * BLK] * lives[j] for j in range(blocks)], axis=0)
    upper = (iota((BLK, BLK), 0) <= iota((BLK, BLK), 1)).astype(F32).astype(BF16)
    summed = dot(jnp.concatenate(split3(masked), axis=0), upper)
    count = blocks * heads
    running_all = summed[:count] + summed[count:2 * count] + summed[2 * count:]
    lane = iota((heads, BLK), 1)
    passed = jnp.zeros((heads, 1), F32)
    for j in range(blocks):
        running = running_all[j * heads:(j + 1) * heads]
        last = running[:, BLK - 1:BLK]
        key_gain[j] = jnp.exp(running - last) * lives[j]
        block_gain[j] = jnp.broadcast_to(jnp.exp(-last), (heads, DH))
        entry_gain[j] = jnp.broadcast_to(jnp.exp(-passed), (heads, DH))
        passed = passed + last
        centre = None
        for b in range(subs):
            middle = running[:, b * SUB + SUB // 2:b * SUB + SUB // 2 + 1]
            doublings = jnp.round(middle * (1.0 / LN2))
            level = doublings * LN2
            row_gain[j, b] = jnp.exp(running - level)
            query_gain[j, b] = jnp.broadcast_to(jnp.exp2(-doublings), (heads, DH)).astype(BF16).astype(F32)
            centre = level if b == 0 else jnp.where(lane >= b * SUB, level, centre)
        low = (DH * EPSILON) * jnp.exp(2.0 * (running - centre))
        floor[j] = jnp.concatenate([low, jnp.zeros((DH - heads, BLK), F32)], axis=0).T
    for h in range(heads):
        decays[h] = jnp.broadcast_to(entry_gain[blocks - 1, h:h + 1, :] * block_gain[blocks - 1, h:h + 1, :], (8, DH))
    states[0] = jnp.zeros(states.shape[1:], F32)

    per_step = [step_rates_ref[i].astype(F32) for i in range(steps)]
    spans = []
    for delta in range(1, steps + 1):
        spans.append([sum(per_step[max(0, i - delta + 1):i + 1]) for i in range(steps)])
    tables = [
        jnp.concatenate([jnp.exp(-spans[delta - 1][i]) if i >= delta else jnp.zeros_like(per_step[0]) for i in range(steps)], axis=0)
        for delta in range(1, steps)
    ]
    tables.append(jnp.concatenate([jnp.exp(-spans[i][i]) for i in range(steps)], axis=0))
    flat = share * steps
    line = iota((flat, 2 * flat), 0)
    column = lax.rem(iota((flat, 2 * flat), 1), flat)
    pick = (column == lax.rem(line, steps) * share + lax.div(line, steps)).astype(F32).astype(BF16)
    for n, table in enumerate(tables):
        top = table.astype(BF16)
        rest = (table - top.astype(F32)).astype(BF16)
        gain_table[n] = dot(pick, jnp.concatenate([top, rest], axis=0))

    def group_cols(g):
        return pl.ds(pl.multiple_of(g * 4 * DH, 4 * DH), 4 * DH)

    def state_lap(j, g):
        rows, cols = block_rows(j), group_cols(g)
        keys, values = kb[rows, cols], vb[rows, cols]
        for one in range(4):
            h = g * 4 + one
            lanes = slice(one * DH, (one + 1) * DH)
            weighted = (keys[:, lanes].T.astype(F32) * key_gain[j, pl.ds(h, 1), :]).astype(BF16)
            states[j + 1, h] = block_gain[j, pl.ds(h, 1), :] * states[j, h] + dot(weighted, values[:, lanes])

    def state_block(j, carry):
        load(0, k_hbm, kb, j).wait()
        load(1, v_hbm, vb, j).wait()

        def state_group(g, carry):
            state_lap(j, g)
            return carry

        return lax.fori_loop(0, groups, state_group, carry)

    decay_copy = pltpu.make_async_remote_copy(
        src_ref=decays, dst_ref=other_decays, send_sem=pair_send_sem.at[2], recv_sem=pair_recv_sem.at[2],
        device_id=(1 - core, me), device_id_type=MESH)
    decay_copy.start()
    lax.fori_loop(0, blocks - 1, state_block, 0)

    load(0, k_hbm, kb, blocks - 1).wait()
    load(1, v_hbm, vb, blocks - 1).wait()

    def send_states(first, n, which):
        some = pl.ds(first, n)
        return pltpu.make_async_remote_copy(
            src_ref=states.at[blocks, some], dst_ref=other_states.at[some], send_sem=pair_send_sem.at[which],
            recv_sem=pair_recv_sem.at[which], device_id=(1 - core, me), device_id_type=MESH)

    for which in range(2):
        first = (1 - core if which == 0 else core) * (groups // 2)

        def last_group(g, carry):
            state_lap(blocks - 1, first + g)
            send_states((first + g) * 4, 4, which).start()
            return carry

        lax.fori_loop(0, groups // 2, last_group, 0)

    for copy in small[3:]:
        copy.wait()
    part = 4 * flat

    def part_rows(p):
        return pl.ds(pl.multiple_of(p * part, part), part)

    def recent_part(p, carry):
        q, k, v = (ref[pl.ds(p * 4, 4)].reshape(part, DH).astype(F32) for ref in (sq, sk, sv))
        own = iota((part, rows_here), 1) == lax.div(iota((part, rows_here), 0), flat) + p * 4

        def gain(n):
            tiled = jnp.concatenate([gain_table[n]] * 4, axis=0)
            return jnp.sum(jnp.where(own, tiled, 0.0), axis=1, keepdims=True)

        total = jnp.sum(q * k, axis=1, keepdims=True) * v
        for delta in range(1, steps):
            affinity = jnp.sum(q * pltpu.roll(k, delta, 0), axis=1, keepdims=True)
            total = total + (affinity * gain(delta - 1)) * pltpu.roll(v, delta, 0)
        recent[part_rows(p), :] = total
        carry_gain[part_rows(p), :] = jnp.broadcast_to(gain(steps - 1), (part, DH))
        return carry

    lax.fori_loop(0, rows_here // 4, recent_part, 0)

    half = BLK // 2
    first_core = core == 0
    per_half = half // SUB

    laps = blocks * groups
    live = [(core * blocks + j < valid_ref[0]).astype(F32) * math.sqrt(DH) for j in range(blocks)]

    def place_of(lap):
        lap = jnp.clip(lap, 0, laps - 1)
        return lax.div(lap, groups), lax.rem(lap, groups)

    def start_scores(lap, twin):
        j, g = place_of(lap)
        rows, cols = block_rows(j), group_cols(g)
        q4, k4 = qb[rows, cols], kb[rows, cols]
        for one in range(4):
            h = g * 4 + one
            lanes = slice(one * DH, (one + 1) * DH)
            q, k = q4[:, lanes], k4[:, lanes]
            for side in range(2):
                here = slice(side * half, (side + 1) * half)
                seen = (side + 1) * half
                scores = dot(q[here], k[:seen], ((1,), (1,)))
                pieces = []
                for b in range(per_half):
                    n = side * per_half + b
                    piece = scores[b * SUB:(b + 1) * SUB] * row_gain[j, n, pl.ds(h, 1), :][:, :seen]
                    causal = iota((SUB, half), 0) + b * SUB >= iota((SUB, half), 1)
                    latest = jnp.where(causal, piece[:, seen - half:], 0.0)
                    scaled = q[here][b * SUB:(b + 1) * SUB].astype(F32) * query_gain[j, n, pl.ds(h, 1), :]
                    pieces.append(jnp.concatenate(([piece[:, :half]] if side else []) + [latest, scaled], axis=1).astype(BF16))
                mixed[twin * 4 + one, :, side * 2 * half:side * 2 * half + seen + half] = jnp.concatenate(pieces, axis=0)

    def apply_values(lap, twin):
        j, g = place_of(lap)
        alive = jnp.where(j == 0, live[0], live[1])
        for n in range(2, blocks):
            alive = jnp.where(j == n, live[n], alive)
        v4 = vb[block_rows(j), group_cols(g)]
        for one in range(4):
            h = g * 4 + one
            v = v4[:, one * DH:(one + 1) * DH]
            prefix = jnp.where(first_core, 0.0, entry_gain[j, pl.ds(h, 1), :] * other_states[h])
            entering = (prefix + states[j, h]).astype(BF16)
            for side in range(2):
                here = slice(side * half, (side + 1) * half)
                seen = (side + 1) * half
                weights = mixed[twin * 4 + one, :, side * 2 * half:side * 2 * half + seen + half]
                mix = dot(weights, jnp.concatenate([v[:seen], entering], axis=0))
                low = jnp.where(iota((half, DH), 1) == h, floor[j, here, :], 0.0)
                scale = lax.rsqrt(jnp.sum(mix * mix + low, axis=1, keepdims=True)) * alive
                out_ref[pl.ds(pl.multiple_of(j * BLK + side * half, half), half), pl.ds(pl.multiple_of(h * DH, DH), DH)] = (
                    mix * scale).astype(BF16)

    def output_lap(lap, carry):
        for twin in range(2):
            apply_values(2 * lap - 2 + twin, twin)
        for twin in range(2):
            start_scores(2 * lap + twin, twin)
        return carry

    def project_group(low, high):
        many = high - low

        def project(quad, carry):
            place = pl.ds(pl.multiple_of(quad * 16, 16), 16)
            x = arrived[low:high, place, :].reshape(many * 16, DH)
            doubled = jnp.concatenate([x, x], axis=1)
            position = lax.div(iota((1, 16, DH), 1), 4)
            chosen = None
            for two in range(2):
                columns = []
                for one in range(2):
                    h = core * share + quad * 4 + two * 2 + one
                    mine, other = states[blocks, h], other_states[h]
                    earlier = jnp.where(first_core, mine, other)
                    latter = jnp.where(first_core, other, mine)
                    decay = jnp.where(first_core, other_decays[h, 0:1, :], decays[h, 0:1, :])
                    final = decay * earlier + latter
                    top = final.astype(BF16)
                    rest = (final - top.astype(F32)).astype(BF16)
                    columns.append(jnp.concatenate([top, rest], axis=0))
                product = dot(doubled, jnp.concatenate(columns, axis=1))
                for one in range(2):
                    piece = product[:, one * DH:(one + 1) * DH].reshape(many, 16, DH)
                    chosen = piece if chosen is None else jnp.where(position == two * 2 + one, piece, chosen)
            projected[low:high, place, :] = chosen.astype(BF16)
            return carry

        lax.fori_loop(0, share // 4, project, 0)

    mixed[...] = jnp.zeros(mixed.shape, BF16)
    decay_copy.wait()
    send_states(pl.multiple_of(core * share, share), share, 0).wait()
    wait_all(slots, arrived, peer_spans[0], 0)
    project_group(0, count_a)
    for n in range(count_a):
        give_back(n).start()

    for j in range(blocks):
        load(2, q_hbm, qb, j).wait()
    send_states(pl.multiple_of((1 - core) * share, share), share, 1).wait()
    lax.fori_loop(0, EARLY, output_lap, 0)

    wait_all(slots, arrived, peer_spans[1], 1)
    project_group(count_a, sessions)
    back[me] = projected[sessions - 1]
    for n in range(count_a, sessions - 1):
        give_back(n).start()

    lax.fori_loop(EARLY, laps // 2 + 1, output_lap, 0)

    wait_all(projected, back, (0, sessions - 1), 2)

    def finish_part(p):
        rows = part_rows(p)
        pieces = [back[session_ref[p * 4 + i]].astype(F32) for i in range(4)]
        reading = carry_gain[rows, :] * jnp.concatenate(pieces, axis=0) + recent[rows, :]
        scale = lax.rsqrt(jnp.mean(reading * reading, axis=1, keepdims=True) + EPSILON)
        decoded_ref[rows, :] = (reading * scale).astype(BF16)

    def finish(p, carry):
        finish_part(p * 2)
        finish_part(p * 2 + 1)
        return carry

    lax.fori_loop(0, rows_here // 8, finish, 0)


def local(side, query_rows, key_rows, value_rows, decay_rates, valid_blocks, step_queries, step_keys, step_values, step_rates, row_session):
    tokens, width = query_rows.shape[1:]
    heads = decay_rates.shape[2]
    blocks = tokens // BLK
    subs = BLK // SUB
    row_count, steps, share_width = step_queries.shape
    share = share_width // DH
    sessions = lax.axis_size("sess")

    def by_head(data):
        return data.reshape(row_count, steps, share, DH).transpose(0, 2, 1, 3).reshape(row_count, share * steps, DH)

    named = row_session[:, 0][None, :] == jnp.arange(sessions, dtype=jnp.int32)[:, None]
    place = jnp.min(jnp.where(named, jnp.arange(row_count, dtype=jnp.int32)[None, :], row_count), axis=1)
    flat_rows = row_count * share * steps

    smem = pl.BlockSpec(memory_space=pltpu.SMEM)
    vmem = pl.BlockSpec(memory_space=pltpu.VMEM)
    hbm = pl.BlockSpec(memory_space=pl.ANY)
    slot = (share * steps, DH)
    dma = pltpu.SemaphoreType.DMA
    prefill_out, decoded = pl.pallas_call(
        functools.partial(fused_kernel, (heads, blocks, sessions, row_count, steps, side)),
        out_shape=(pltpu.VMEM((tokens, width), BF16), pltpu.VMEM((flat_rows, DH), BF16)),
        in_specs=[smem, smem, smem] + [hbm] * 8,
        out_specs=(vmem, vmem),
        scratch_shapes=[
            pltpu.VMEM((tokens, width), BF16), pltpu.VMEM((tokens, width), BF16), pltpu.VMEM((tokens, width), BF16),
            pltpu.VMEM((heads, tokens), F32), pltpu.VMEM((steps, share, row_count), BF16),
            pltpu.VMEM((row_count,) + slot, BF16), pltpu.VMEM((row_count,) + slot, BF16), pltpu.VMEM((row_count,) + slot, BF16),
            pltpu.VMEM((sessions,) + slot, BF16), pltpu.VMEM((sessions,) + slot, BF16),
            pltpu.VMEM((sessions,) + slot, BF16), pltpu.VMEM((sessions,) + slot, BF16),
            pltpu.VMEM((flat_rows, DH), F32), pltpu.VMEM((flat_rows, DH), F32), pltpu.VMEM((steps, share * steps, row_count), F32),
            pltpu.VMEM((blocks + 1, heads, DH, DH), F32), pltpu.VMEM((heads, DH, DH), F32),
            pltpu.VMEM((heads, 8, DH), F32), pltpu.VMEM((heads, 8, DH), F32),
            pltpu.VMEM((blocks, heads, BLK), F32), pltpu.VMEM((blocks, heads, DH), F32), pltpu.VMEM((blocks, heads, DH), F32),
            pltpu.VMEM((blocks, subs, heads, BLK), F32), pltpu.VMEM((blocks, subs, heads, DH), F32),
            pltpu.VMEM((blocks, BLK, DH), F32), pltpu.VMEM((8, BLK // 2, 5 * BLK // 2), BF16),
            dma((3, blocks)), dma((5,)), dma((3,)), dma((3,)), dma((3,)), dma((3,)),
        ],
        compiler_params=pltpu.CompilerParams(collective_id=0, has_side_effects=True, vmem_limit_bytes=48 << 20),
    )(valid_blocks, place, row_session[:, 0], decay_rates[0].T, step_rates.transpose(1, 2, 0), query_rows[0], key_rows[0], value_rows[0],
      by_head(step_queries), by_head(step_keys), by_head(step_values))
    decode_out = decoded.reshape(row_count, share, steps, DH).transpose(0, 2, 1, 3).reshape(row_count, steps, share_width)
    return prefill_out[None], decode_out


def solution(mesh):
    long, step = P("sess", "ctx", None), P("sess", None, "ctx")
    devices = mesh.shape["sess"]
    side = round(devices ** (1 / 3))
    sides = (side, side, side) if side ** 3 == devices else (1, 1, devices)
    return jax.shard_map(
        functools.partial(local, sides),
        mesh=mesh,
        in_specs=(long, long, long, long, P("sess"), step, step, step, step, P("sess", None)),
        out_specs=(long, step),
        check_vma=False,
    )
```
